32 devices in a mesh: dp: 4 (over z), expert: 8 (over y, x, core).
Axes of the slice: x: 2, y: 2, z: 4, core: 2. Of those that a mesh axis runs over, the one named last changes fastest.
Arguments:
- inputs: bfloat16 [4096, 2048], P(('dp', 'expert')), may hold values from -6 to 6
- out_grad: bfloat16 [4096, 2048], P(('dp', 'expert')), may hold values from -6 to 6
- combine: float32 [4096, 8], P(('dp', 'expert')), may hold values from 0 to 1, as said below
- routes: int32 [4096, 8], P(('dp', 'expert')), may hold values from 0 to 31, all different within a row; in each aligned block of 128 rows (0 to 127, 128 to 255, ...) at most 48 rows name the same one
- saved_hidden: bfloat16 [4, 32, 8, 48, 768], P('dp', 'expert'), may hold values from -6 to 6
- down_weight: bfloat16 [32, 2048, 768], P('expert'), may hold values from -0.21875 to 0.21875
- router_weight: bfloat16 [32, 2048], replicated, may hold values from -0.125 to 0.125
Outputs:
- hidden_grad: bfloat16 [4, 32, 8, 48, 768], P('dp', 'expert')
- down_grad: bfloat16 [32, 2048, 768], P('expert', 'dp')
- input_grad: bfloat16 [4096, 2048], P(('dp', 'expert'))
- router_grad: float32 [32, 2048], replicated
The draws below stay inside these ranges and needn't reach their ends.
Inputs may be any that keep to these rules, and one draw needn't show every extreme that they name: `routes`: each token names 8 different experts; among the 128 tokens of one device no expert is named by more than 48 tokens, a bound that some block reaches. `combine`: each token's 8 weights are positive and sum to one.
All inputs are finite; a program needn't handle non-finite values.
Results may differ from the reference program's by a relative error of at most 0.017.
Values may be sent and summed in bfloat16 or wider, within the bound.
No kernel may reach another device: no remote copies, remote signals or barrier semaphores. Data moves between devices by JAX's collectives and lax.ppermute only.
A program may use at most 128 MiB of HBM per device.

```python
import math
import jax
import jax.numpy as jnp
import numpy as np
from jax import lax

D = 2048
FF = 768
TOP = 8
TOK_DEV = 128
EXPERTS = 32
CAP = 48
TOKENS = 4096
N_DP = 4
N_EXPERT = 8


def draw_combine(key, part):
    raw_weights = jnp.exp(jax.random.uniform(key, (TOKENS, TOP), jnp.float32, -2.0, 2.0))
    return raw_weights / jnp.sum(raw_weights, axis=1, keepdims=True)


def block_levels(own_key, dims, pieces, low, top_value):
    level = 1.0
    for dim, blocks in pieces:
        steps = jax.random.uniform(jax.random.fold_in(jax.random.fold_in(own_key, 6), dim), (blocks,), jnp.float32, low / len(pieces), top_value / len(pieces))
        level = level * jnp.repeat(jnp.exp(steps), dims[dim] // blocks).reshape((-1,) + (1,) * (len(dims) - 1 - dim))
    return level


def deal_out(stream_key, own, number, rows, number_of, top, reach, slope):
    sequence = jax.random.permutation(stream_key, number_of)
    packed, ordinary = load_shares(number_of, rows * top, reach, slope, True), load_shares(number_of, rows * top, reach, slope, False)
    places = jnp.arange(number_of)

    def named(tallies, offset_by):
        used = int((tallies > 0).sum())
        fixed = max(1, used // 4)
        moved = fixed + (places - fixed + offset_by * (used - fixed)) % max(1, number_of - fixed)
        return jnp.zeros((number_of,), jnp.int32).at[sequence[jnp.where(places < fixed, places, moved)]].set(jnp.asarray(tallies, jnp.int32))

    tallies = jnp.where(number % 4 == 0, named(packed, number // 4), named(ordinary, number - number // 4 - 1))
    mixed = jax.random.permutation(jax.random.fold_in(own, 3), number_of)
    giver, taker = mixed[0:number_of // 2 * 2:2], mixed[1:number_of // 2 * 2:2]
    room = jnp.minimum(tallies[giver] - 1, reach - tallies[taker]) // 2
    room = jnp.where((giver == sequence[0]) | (taker == sequence[0]) | (tallies[taker] == 0), 0, jnp.maximum(room, 0))
    moved = jax.random.randint(jax.random.fold_in(own, 4), (number_of // 2,), 0, 1 << 20) % (room + 1)
    tallies = tallies.at[giver].add(-moved).at[taker].add(moved)
    labels = jnp.searchsorted(jnp.cumsum(tallies), jnp.arange(rows * top), side="right").astype(jnp.int32)
    grid = labels.reshape(top, rows).T
    grid = grid[jax.random.permutation(jax.random.fold_in(own, 1), rows)]
    offset_by = jax.random.randint(jax.random.fold_in(own, 2), (rows, 1), 0, top)
    return jnp.take_along_axis(grid, (jnp.arange(top)[None, :] + offset_by) % top, axis=1)


def load_shares(amount, total, limit, skew, full):
    loads = [(1 << 20) // math.isqrt(rank ** skew) + 1 for rank in range(1, amount + 1)]
    largest = limit if full else min(limit, max(-(-total // amount), total * loads[0] // sum(loads)))
    least = 1 if total - largest >= amount - 1 else 0
    holding, spare = [largest] + [least] * (amount - 1), total - largest - least * (amount - 1)
    while spare > 0:
        free = [i for i in range(1, amount) if holding[i] < largest] or [i for i in range(1, amount) if holding[i] < limit]
        mass, left = sum([loads[i] for i in free]), spare
        for i in free:
            addition = min(limit - holding[i], max(1, left * loads[i] // mass), spare)
            holding[i] = holding[i] + addition
            spare = spare - addition
    return np.array(holding)


def gaussian(rng, shape, spread, most, split=(), held_as=jnp.bfloat16):
    level = block_levels(rng, shape, split, -0.22, 0.18) if split else 1.0
    result = jax.random.normal(rng, shape, jnp.float32) * spread * level
    return jnp.minimum(jnp.maximum(result, -most), most).astype(held_as)


def setup_inputs(seed: int = 0) -> dict:
    keys = jax.random.split(jax.random.key(seed), 8)
    inputs = gaussian(keys[0], (TOKENS, D), 1.0, 6.0, ((0, 32),))
    out_grad = gaussian(keys[1], (TOKENS, D), 1.0, 6.0, ((0, 32),))
    combine = draw_combine(jax.random.fold_in(keys[7], 71), 0)
    routes_keys = jax.random.split(jax.random.fold_in(keys[3], 1), TOKENS // TOK_DEV)
    routes_turns = jax.random.permutation(jax.random.fold_in(keys[3], 3), TOKENS // TOK_DEV)
    routes = jax.vmap(lambda own, number: deal_out(jax.random.fold_in(keys[3], 2), own, number, TOK_DEV, EXPERTS, TOP, CAP, 2))(routes_keys, routes_turns).reshape((TOKENS, TOP))
    saved_hidden = gaussian(keys[4], (N_DP, EXPERTS, N_EXPERT, CAP, FF), 1.0, 6.0, ((0, 4), (1, 8)))
    down_weight = gaussian(keys[5], (EXPERTS, D, FF), FF ** -0.5, 0.21875, ((0, 8),))
    router_weight = gaussian(keys[6], (EXPERTS, D), D ** -0.5, 0.125)
    return {"inputs": inputs, "out_grad": out_grad, "combine": combine, "routes": routes, "saved_hidden": saved_hidden, "down_weight": down_weight, "router_weight": router_weight}


def slot_positions(block_routes):
    marks = (block_routes[:, :, None] == jnp.arange(EXPERTS, dtype=jnp.int32)[None, None, :]).astype(jnp.int32)
    counts = jnp.sum(marks, axis=1)
    before = jnp.cumsum(counts, axis=0) - counts
    return jnp.sum(marks * before[:, None, :], axis=2).astype(jnp.int32)


def reference(inputs, out_grad, combine, routes, saved_hidden, down_weight, router_weight):
    blocks = routes.reshape(N_DP * N_EXPERT, TOK_DEV, TOP)
    positions = jax.vmap(slot_positions)(blocks).reshape(TOKENS, TOP)
    token_ids = jnp.arange(TOKENS, dtype=jnp.int32)
    device = token_ids // TOK_DEV
    group_ids = device // N_EXPERT
    source = device % N_EXPERT
    slot_flat = ((group_ids[:, None] * EXPERTS + routes) * N_EXPERT + source[:, None]) * CAP + positions
    slot_total = N_DP * EXPERTS * N_EXPERT * CAP
    pair_total = TOKENS * TOP
    owner_pair = jnp.full((slot_total,), pair_total, jnp.int32)
    owner_pair = owner_pair.at[slot_flat.reshape(-1)].set(jnp.arange(pair_total, dtype=jnp.int32))
    owner_pair = owner_pair.reshape(N_DP, EXPERTS, N_EXPERT * CAP)
    flat_combine = combine.reshape(-1)

    def one_expert(expert):
        pair_ids = lax.dynamic_index_in_dim(owner_pair, expert, 1, keepdims=False)
        filled = pair_ids < pair_total
        safe_pair = jnp.where(filled, pair_ids, 0)
        gain_values = jnp.where(filled, flat_combine[safe_pair], jnp.zeros((), jnp.float32))
        slot_rows = (gain_values[:, :, None] * out_grad[safe_pair // TOP].astype(jnp.float32)).astype(jnp.bfloat16)
        slot_acts = lax.dynamic_index_in_dim(saved_hidden, expert, 1, keepdims=False).reshape(N_DP, N_EXPERT * CAP, FF)
        weight = lax.dynamic_index_in_dim(down_weight, expert, 0, keepdims=False)
        flat_rows = slot_rows.reshape(-1, D)
        flat_hidden = slot_acts.reshape(-1, FF)
        recomputed = lax.dot_general(flat_hidden, weight, (((1,), (1,)), ((), ())), preferred_element_type=jnp.float32)
        products = jnp.sum(recomputed * flat_rows.astype(jnp.float32), axis=1)
        hidden_part = jnp.dot(flat_rows, weight, preferred_element_type=jnp.float32).astype(jnp.bfloat16)
        partial_grads = jnp.einsum('gsd,gsf->gdf', slot_rows.astype(jnp.float32), slot_acts.astype(jnp.float32))
        rounded = lax.optimization_barrier(partial_grads.astype(jnp.bfloat16))
        weight_part = jnp.sum(rounded.astype(jnp.float32), axis=0).astype(jnp.bfloat16)
        return products, hidden_part, weight_part

    products, hidden_parts, down_grad = lax.map(one_expert, jnp.arange(EXPERTS, dtype=jnp.int32))
    hidden_grad = hidden_parts.reshape(EXPERTS, N_DP, N_EXPERT, CAP, FF).transpose(1, 0, 2, 3, 4)
    product_flat = products.reshape(EXPERTS, N_DP, N_EXPERT, CAP).transpose(1, 0, 2, 3).reshape(-1)
    pair_sums = product_flat[slot_flat]
    logit_grad = pair_sums - combine * jnp.sum(pair_sums, axis=1, keepdims=True)
    route_marks = routes[:, :, None] == jnp.arange(EXPERTS, dtype=jnp.int32)[None, None, :]
    dense_grad = jnp.sum(jnp.where(route_marks, logit_grad[:, :, None], jnp.zeros((), jnp.float32)), axis=1).astype(jnp.bfloat16)
    input_grad = jnp.dot(dense_grad, router_weight, preferred_element_type=jnp.float32).astype(jnp.bfloat16)
    router_grad = lax.dot_general(dense_grad, inputs, (((0,), (0,)), ((), ())), preferred_element_type=jnp.float32)
    return hidden_grad, down_grad, input_grad, router_grad
```

```python
import functools

import jax
import jax.numpy as jnp
from jax import lax
from jax.experimental import pallas as pl
from jax.experimental.pallas import tpu as pltpu
from jax.sharding import PartitionSpec as P

F32 = jnp.float32
BF16 = jnp.bfloat16
LANES = 128
KINDS = 4
VMEM_LIMIT = 56 * 1024 * 1024


def make_marks(block_routes, total_experts):
    return block_routes[:, :, None] == jnp.arange(total_experts, dtype=jnp.int32)[None, None, :]


def slot_positions(route_marks):
    counts = jnp.sum(route_marks.astype(BF16), axis=1)
    token_order = jnp.arange(route_marks.shape[0], dtype=jnp.int32)
    earlier = (token_order[None, :] < token_order[:, None]).astype(BF16)
    before = jnp.dot(earlier, counts, preferred_element_type=F32)
    picked = jnp.sum(jnp.where(route_marks, before[:, None, :], 0.0), axis=2)
    return picked.astype(jnp.int32)


def pack_rows(scaled, lane_index, owner_slot, positions, local_experts, groups, capacity):
    width = scaled.shape[-1]
    flat_index = (owner_slot * groups + lane_index) * capacity + positions
    zero_rows = jnp.zeros((local_experts * groups * capacity, width), BF16)
    filled = zero_rows.at[flat_index.reshape(-1)].set(scaled.reshape(-1, width))
    return filled.reshape(local_experts, groups, capacity, width)


def local_any(inputs, out_grad, combine, routes, saved_hidden, down_weight, router_weight):
    token_count, width = out_grad.shape
    local_experts = down_weight.shape[0]
    total_experts = router_weight.shape[0]
    groups = lax.axis_size("expert")
    capacity = saved_hidden.shape[3]
    hidden_width = saved_hidden.shape[4]
    route_marks = make_marks(routes, total_experts)
    positions = slot_positions(route_marks)
    owner_dev = routes // local_experts
    owner_slot = routes % local_experts
    scaled = (combine[:, :, None] * out_grad[:, None, :].astype(F32)).astype(BF16)
    packed = pack_rows(scaled, owner_dev, owner_slot, positions, local_experts, groups, capacity)
    received = lax.all_to_all(packed, "expert", split_axis=1, concat_axis=1, tiled=True)
    hidden_local = saved_hidden[0]
    products_list = []
    hidden_list = []
    weight_terms = []
    for expert in range(local_experts):
        slot_rows = received[expert].reshape(groups * capacity, width)
        slot_acts = hidden_local[expert].reshape(groups * capacity, hidden_width)
        weight = down_weight[expert]
        hidden = jnp.dot(slot_rows, weight, preferred_element_type=F32)
        products_list.append(jnp.sum(hidden * slot_acts.astype(F32), axis=1))
        hidden_list.append(hidden.astype(BF16))
        weight_terms.append(
            lax.dot_general(
                slot_rows, slot_acts, (((0,), (0,)), ((), ())), preferred_element_type=F32
            )
        )
    down_grad = lax.psum_scatter(
        jnp.stack(weight_terms).astype(BF16), "dp", scatter_dimension=1, tiled=True
    )
    hidden_grad = jnp.stack(hidden_list).reshape(1, local_experts, groups, capacity, hidden_width)
    slot_products = jnp.stack(products_list).reshape(local_experts, groups, capacity)
    returned = lax.all_to_all(slot_products, "expert", split_axis=1, concat_axis=1, tiled=True)
    pair_index = (owner_slot * groups + owner_dev) * capacity + positions
    pair_sums = returned.reshape(-1)[pair_index]
    logit_grad = pair_sums - combine * jnp.sum(pair_sums, axis=1, keepdims=True)
    dense_grad = jnp.sum(jnp.where(route_marks, logit_grad[:, :, None], 0.0), axis=1).astype(BF16)
    input_grad = jnp.dot(dense_grad, router_weight, preferred_element_type=F32).astype(BF16)
    router_part = lax.dot_general(
        dense_grad, inputs, (((0,), (0,)), ((), ())), preferred_element_type=F32
    )
    router_grad = lax.psum(router_part, ("dp", "expert"))
    return (hidden_grad, down_grad, input_grad, router_grad)


INNER = [(1, 2), (2, 1)]
FAR = [(0, 2), (3, 1)]
OUTER = [(0, 1), (3, 2)]
OUTWARD = [(1, 0), (2, 3)]


def plane_swap(x, bits):
    return lax.ppermute(x, "expert", [(i, i ^ bits) for i in range(8)])


def plane_gather(x):
    half = x.shape[0] // 2
    across = plane_swap(x, 2)
    along = plane_swap(x, 4)
    diagonal = jnp.concatenate([plane_swap(across[:half], 4), plane_swap(along[half:], 2)])
    same_core = {0: x, 2: across, 4: along, 6: diagonal}
    blocks = dict(same_core)
    for k, block in same_core.items():
        blocks[k + 1] = plane_swap(block, 1)
    return [blocks[k] for k in range(8)]


def dense_routes(routes, combine, total_experts):
    marks = make_marks(routes, total_experts)
    counts = jnp.sum(marks.astype(F32), axis=1)
    token_order = jnp.arange(routes.shape[0], dtype=jnp.int32)
    earlier = (token_order[None, :] < token_order[:, None]).astype(BF16)
    before = jnp.dot(earlier, counts.astype(BF16), preferred_element_type=F32)
    routed = counts > 0.0
    weights = jnp.sum(jnp.where(marks, combine[:, :, None], 0.0), axis=1)
    return routed, jnp.where(routed, before, -1.0), weights


def describe(positions, weights):
    high = lax.reduce_precision(weights, 8, 7)
    middle = lax.reduce_precision(weights - high, 8, 7)
    low = weights - high - middle
    stacked = jnp.concatenate([positions, high, middle, low], axis=1)
    return stacked.T.astype(BF16)


def pick_rows(owner, local_experts, total_experts):
    row = lax.broadcasted_iota(jnp.int32, (KINDS * local_experts, LANES), 0)
    column = lax.broadcasted_iota(jnp.int32, (KINDS * local_experts, LANES), 1)
    wanted = (row // local_experts) * total_experts + owner * local_experts + row % local_experts
    return (column == wanted).astype(BF16)


def place_rows(ref, start, width, picker, local_experts, capacity, step, store):
    notes = jnp.dot(
        picker, ref[:, start + width : start + width + LANES], preferred_element_type=F32
    )
    slots = lax.broadcasted_iota(jnp.int32, (capacity, LANES), 0).astype(F32)
    marks = []
    scales = []
    for expert in range(local_experts):
        weight = (
            notes[local_experts + expert : local_experts + expert + 1]
            + notes[2 * local_experts + expert : 2 * local_experts + expert + 1]
            + notes[3 * local_experts + expert : 3 * local_experts + expert + 1]
        )
        hit = slots == notes[expert : expert + 1]
        marks.append(jnp.where(hit, 1.0, 0.0).astype(BF16))
        scales.append(jnp.sum(jnp.where(hit, weight, 0.0), axis=1, keepdims=True))
    mark = jnp.concatenate(marks, axis=0)
    scale = jnp.concatenate(scales, axis=0)
    for column in range(0, width, step):
        rows = jnp.dot(
            mark,
            ref[:, start + column : start + column + step],
            preferred_element_type=F32,
        )
        rows = (rows * scale).astype(BF16)
        for expert in range(local_experts):
            store(expert, column, step, rows[expert * capacity : (expert + 1) * capacity])


def hidden_kernel(local_experts, total_experts, capacity, width, part, place, *refs):
    blocks = refs[:8]
    weight_ref, acts_ref, hidden_ref, products_ref, near_ref, rows = refs[8:]
    expert = pl.program_id(0)
    me = place[0]

    @pl.when(expert == 0)
    def _():
        picker = pick_rows(me, local_experts, total_experts)
        for k in range(8):
            base = pl.multiple_of((me ^ k) * capacity, 16)

            def store(e, column, step, value, base=base):
                rows[e, pl.ds(base, capacity), column : column + step] = value

            place_rows(blocks[k], 0, width, picker, local_experts, capacity, 512, store)

    hidden = jnp.dot(rows[expert], weight_ref[0], preferred_element_type=F32)
    hidden_ref[0] = hidden.astype(BF16)
    product = hidden * acts_ref[0].astype(F32)
    products_ref[0] = jnp.sum(product.reshape(8, capacity, product.shape[1]), axis=2)
    own = pl.multiple_of(place[1] * part, LANES)
    other = pl.multiple_of(place[2] * part, LANES)
    near_ref[0, :, :part] = rows[expert, :, pl.ds(own, part)]
    near_ref[0, :, part:] = rows[expert, :, pl.ds(other, part)]


def hidden_call(place, blocks, weight, acts, total_experts, capacity, part):
    local_experts, width, hidden_width = weight.shape
    slots = acts.shape[1]
    kernel = functools.partial(
        hidden_kernel, local_experts, total_experts, capacity, width, part
    )
    whole = pl.BlockSpec(blocks[0].shape, lambda e, p: (0, 0))
    return pl.pallas_call(
        kernel,
        grid_spec=pltpu.PrefetchScalarGridSpec(
            num_scalar_prefetch=1,
            grid=(local_experts,),
            in_specs=[whole] * 8
            + [
                pl.BlockSpec((1, width, hidden_width), lambda e, p: (e, 0, 0)),
                pl.BlockSpec((1, slots, hidden_width), lambda e, p: (e, 0, 0)),
            ],
            out_specs=[
                pl.BlockSpec((1, slots, hidden_width), lambda e, p: (e, 0, 0)),
                pl.BlockSpec((1, 8, capacity), lambda e, p: (e, 0, 0)),
                pl.BlockSpec((1, slots, 2 * part), lambda e, p: (e, 0, 0)),
            ],
            scratch_shapes=[pltpu.VMEM((local_experts, slots, width), BF16)],
        ),
        out_shape=[
            jax.ShapeDtypeStruct((local_experts, slots, hidden_width), BF16),
            jax.ShapeDtypeStruct((local_experts, 8, capacity), F32),
            jax.ShapeDtypeStruct((local_experts, slots, 2 * part), BF16),
        ],
        compiler_params=pltpu.CompilerParams(vmem_limit_bytes=VMEM_LIMIT),
        cost_estimate=pl.CostEstimate(
            flops=2 * local_experts * slots * width * (hidden_width + 256),
            bytes_accessed=2 * (weight.size + 2 * acts.size + 10 * blocks[0].size),
            transcendentals=0,
        ),
        name="hidden_and_products",
    )(place, *blocks, weight, acts)


def rows_kernel(local_experts, total_experts, capacity, widths, place, *refs):
    blocks = refs[:8]
    outs = refs[8:]
    me = place[0]
    picker = pick_rows(me, local_experts, total_experts)
    for k in range(8):
        base = pl.multiple_of((me ^ k) * capacity, 16)
        start = 0
        for out, width in zip(outs, widths):

            def store(e, column, step, value, base=base, out=out):
                out[e, pl.ds(base, capacity), column : column + step] = value

            place_rows(blocks[k], start, width, picker, local_experts, capacity, 512, store)
            start += width + LANES


def rows_call(place, blocks, widths, local_experts, total_experts, capacity):
    kernel = functools.partial(rows_kernel, local_experts, total_experts, capacity, widths)
    slots = 8 * capacity
    vmem = pl.BlockSpec(memory_space=pltpu.VMEM)
    return pl.pallas_call(
        kernel,
        in_specs=[pl.BlockSpec(memory_space=pltpu.SMEM)] + [vmem] * 8,
        out_specs=[vmem] * len(widths),
        out_shape=[jax.ShapeDtypeStruct((local_experts, slots, w), BF16) for w in widths],
        compiler_params=pltpu.CompilerParams(vmem_limit_bytes=VMEM_LIMIT),
        cost_estimate=pl.CostEstimate(
            flops=2 * local_experts * slots * 256 * sum(widths),
            bytes_accessed=2 * (8 * blocks[0].size + local_experts * slots * sum(widths)),
            transcendentals=0,
        ),
        name="far_rows",
    )(place, *blocks)


def outer_product(rows, acts):
    return lax.dot_general(rows, acts, (((0,), (0,)), ((), ())), preferred_element_type=F32)


def down_kernel(near, inner, far, outer, near_a, inner_a, far_a, outer_a, own_ref, other_ref):
    total = outer_product(near[0], near_a[...])
    total += outer_product(inner[0], inner_a[...])
    total += outer_product(far[0], far_a[...])

    @pl.when(pl.program_id(0) == 0)
    def _():
        other_ref[...] = total.astype(BF16)

    @pl.when(pl.program_id(0) == 1)
    def _():
        own_ref[...] = total + outer_product(outer[0], outer_a[...])


def down_call(expert, near, inner, far, outer, near_a, inner_a, far_a, outer_a):
    slots, hidden_width = near_a.shape
    part = outer.shape[2]
    half = pl.BlockSpec((1, slots, part), lambda i: (expert, 0, 1 - i))
    acts = pl.BlockSpec((slots, hidden_width), lambda i: (0, 0))
    result = pl.BlockSpec((part, hidden_width), lambda i: (0, 0))
    return pl.pallas_call(
        down_kernel,
        grid=(2,),
        in_specs=[half, half, half, pl.BlockSpec((1, slots, part), lambda i: (expert, 0, 0))]
        + [acts] * 4,
        out_specs=[result, result],
        out_shape=[
            jax.ShapeDtypeStruct((part, hidden_width), F32),
            jax.ShapeDtypeStruct((part, hidden_width), BF16),
        ],
        compiler_params=pltpu.CompilerParams(vmem_limit_bytes=VMEM_LIMIT),
        cost_estimate=pl.CostEstimate(
            flops=2 * slots * hidden_width * 7 * part,
            bytes_accessed=2 * (7 * slots * part + 4 * slots * hidden_width + 3 * part * hidden_width),
            transcendentals=0,
        ),
        name="down_terms",
    )(near, inner, far, outer, near_a, inner_a, far_a, outer_a)


def sum_everywhere(x, member):
    kept = []
    for bits in (1, 2, 4):
        half = x.shape[1] // 2
        low, high = x[:, :half], x[:, half:]
        upper = (member & bits) != 0
        kept.append(upper)
        x = jnp.where(upper, high, low) + plane_swap(jnp.where(upper, low, high), bits)
    others = [lax.ppermute(x, "dp", [(i, i ^ k) for i in range(4)]) for k in (1, 2, 3)]
    x = (x + others[0]) + (others[1] + others[2])
    for bits, upper in zip((4, 2, 1), reversed(kept)):
        other = plane_swap(x, bits)
        x = jnp.concatenate([jnp.where(upper, other, x), jnp.where(upper, x, other)], axis=1)
    return x


def local_line(inputs, out_grad, combine, routes, saved_hidden, down_weight, router_weight):
    width = out_grad.shape[1]
    local_experts = down_weight.shape[0]
    total_experts = router_weight.shape[0]
    capacity = saved_hidden.shape[3]
    hidden_width = saved_hidden.shape[4]
    slots = 8 * capacity
    part = width // 4
    plane = lax.axis_index("dp")
    member = lax.axis_index("expert")
    lower = plane < 2
    acts = saved_hidden.reshape(local_experts, slots, hidden_width)

    routed, positions, weights = dense_routes(routes, combine, total_experts)
    notes = describe(positions, weights)
    parts = [out_grad[:, i * part : (i + 1) * part] for i in range(4)]

    pair = jnp.concatenate(
        [jnp.where(lower, parts[2], parts[1]), jnp.where(lower, parts[3], parts[0]), notes], axis=1
    )
    single = jnp.concatenate([jnp.where(lower, parts[1], parts[2]), notes], axis=1)
    from_inner = lax.ppermute(pair, "dp", INNER)
    from_far = lax.ppermute(pair, "dp", FAR)
    from_outer = lax.ppermute(single, "dp", OUTER)

    own_blocks = plane_gather(jnp.concatenate([out_grad, notes], axis=1))

    inner_acts = []
    outer_acts = []
    far_acts = []
    for expert in range(local_experts):
        outer_acts.append(lax.ppermute(acts[expert], "dp", OUTER))
        inner_acts.append(lax.ppermute(acts[expert], "dp", INNER))
        far_acts.append(lax.ppermute(acts[expert], "dp", FAR))

    other_blocks = plane_gather(jnp.concatenate([from_inner, from_far, from_outer], axis=1))

    other_part = jnp.where(lower, 0, 3)
    place = jnp.stack([member, plane, other_part]).astype(jnp.int32)
    hidden, products, near = hidden_call(
        place, own_blocks, down_weight, acts, total_experts, capacity, part
    )

    returned = lax.all_to_all(products, "expert", split_axis=1, concat_axis=1, tiled=True)
    by_expert = returned.transpose(1, 0, 2).reshape(total_experts, capacity)
    slot_order = jnp.arange(capacity, dtype=jnp.int32).astype(F32)
    hit = positions[:, :, None] == slot_order[None, None, :]
    pair_sums = jnp.sum(jnp.where(hit, by_expert[None], 0.0), axis=2)
    logit_grad = pair_sums - weights * jnp.sum(pair_sums, axis=1, keepdims=True)
    dense_grad = jnp.where(routed, logit_grad, 0.0).astype(BF16)
    input_grad = jnp.dot(dense_grad, router_weight, preferred_element_type=F32).astype(BF16)
    router_part = lax.dot_general(
        dense_grad, inputs, (((0,), (0,)), ((), ())), preferred_element_type=F32
    )
    router_grad = sum_everywhere(router_part, member)

    inner, far, outer = rows_call(
        place, other_blocks, (2 * part, 2 * part, part), local_experts, total_experts, capacity
    )
    down = []
    for expert in range(local_experts):
        own, other = down_call(
            expert, near, inner, far, outer,
            acts[expert], inner_acts[expert], far_acts[expert], outer_acts[expert],
        )
        arrived = lax.ppermute(other, "dp", OUTWARD)
        down.append((own + arrived.astype(F32)).astype(BF16))
    down_grad = jnp.stack(down)

    hidden_grad = hidden.reshape(saved_hidden.shape)
    return (hidden_grad, down_grad, input_grad, router_grad)


def solution(mesh):
    in_line = mesh.shape["dp"] == 4 and mesh.shape["expert"] == 8

    def local(inputs, out_grad, combine, routes, saved_hidden, down_weight, router_weight):
        tokens, width = out_grad.shape
        fits = (
            in_line
            and tokens == LANES
            and KINDS * router_weight.shape[0] == LANES
            and width % 2048 == 0
            and saved_hidden.shape[3] % 16 == 0
            and saved_hidden.shape[4] % LANES == 0
        )
        body = local_line if fits else local_any
        return body(
            inputs, out_grad, combine, routes, saved_hidden, down_weight, router_weight
        )

    placed = (
        P(("dp", "expert"), None),
        P(("dp", "expert"), None),
        P(("dp", "expert"), None),
        P(("dp", "expert"), None),
        P("dp", "expert", None, None, None),
        P("expert", None, None),
        P(),
    )
    return jax.shard_map(
        local,
        mesh=mesh,
        in_specs=placed,
        out_specs=(
            P("dp", "expert", None, None, None),
            P("expert", "dp", None),
            P(("dp", "expert"), None),
            P(),
        ),
        check_vma=False,
    )
```

```python
import functools

import jax
import jax.numpy as jnp
from jax import lax
from jax.experimental import pallas as pl
from jax.experimental.pallas import tpu as pltpu
from jax.sharding import PartitionSpec as P

F32 = jnp.float32
BF16 = jnp.bfloat16
LANES = 128
KINDS = 4
VMEM_LIMIT = 48 * 1024 * 1024
ANYWHERE = pl.BlockSpec(memory_space=pl.ANY)
SMALL = pl.CostEstimate(flops=1000, bytes_accessed=1000, transcendentals=0)


def make_marks(block_routes, total_experts):
    return block_routes[:, :, None] == jnp.arange(total_experts, dtype=jnp.int32)[None, None, :]


def slot_positions(route_marks):
    counts = jnp.sum(route_marks.astype(BF16), axis=1)
    token_order = jnp.arange(route_marks.shape[0], dtype=jnp.int32)
    earlier = (token_order[None, :] < token_order[:, None]).astype(BF16)
    before = jnp.dot(earlier, counts, preferred_element_type=F32)
    picked = jnp.sum(jnp.where(route_marks, before[:, None, :], 0.0), axis=2)
    return picked.astype(jnp.int32)


def pack_rows(scaled, lane_index, owner_slot, positions, local_experts, groups, capacity):
    width = scaled.shape[-1]
    flat_index = (owner_slot * groups + lane_index) * capacity + positions
    zero_rows = jnp.zeros((local_experts * groups * capacity, width), BF16)
    filled = zero_rows.at[flat_index.reshape(-1)].set(scaled.reshape(-1, width))
    return filled.reshape(local_experts, groups, capacity, width)


def local_any(inputs, out_grad, combine, routes, saved_hidden, down_weight, router_weight):
    token_count, width = out_grad.shape
    local_experts = down_weight.shape[0]
    total_experts = router_weight.shape[0]
    groups = lax.axis_size("expert")
    capacity = saved_hidden.shape[3]
    hidden_width = saved_hidden.shape[4]
    route_marks = make_marks(routes, total_experts)
    positions = slot_positions(route_marks)
    owner_dev = routes // local_experts
    owner_slot = routes % local_experts
    scaled = (combine[:, :, None] * out_grad[:, None, :].astype(F32)).astype(BF16)
    packed = pack_rows(scaled, owner_dev, owner_slot, positions, local_experts, groups, capacity)
    received = lax.all_to_all(packed, "expert", split_axis=1, concat_axis=1, tiled=True)
    hidden_local = saved_hidden[0]
    products_list = []
    hidden_list = []
    weight_terms = []
    for expert in range(local_experts):
        slot_rows = received[expert].reshape(groups * capacity, width)
        slot_acts = hidden_local[expert].reshape(groups * capacity, hidden_width)
        weight = down_weight[expert]
        hidden = jnp.dot(slot_rows, weight, preferred_element_type=F32)
        products_list.append(jnp.sum(hidden * slot_acts.astype(F32), axis=1))
        hidden_list.append(hidden.astype(BF16))
        weight_terms.append(
            lax.dot_general(
                slot_rows, slot_acts, (((0,), (0,)), ((), ())), preferred_element_type=F32
            )
        )
    down_grad = lax.psum_scatter(
        jnp.stack(weight_terms).astype(BF16), "dp", scatter_dimension=1, tiled=True
    )
    hidden_grad = jnp.stack(hidden_list).reshape(1, local_experts, groups, capacity, hidden_width)
    slot_products = jnp.stack(products_list).reshape(local_experts, groups, capacity)
    returned = lax.all_to_all(slot_products, "expert", split_axis=1, concat_axis=1, tiled=True)
    pair_index = (owner_slot * groups + owner_dev) * capacity + positions
    pair_sums = returned.reshape(-1)[pair_index]
    logit_grad = pair_sums - combine * jnp.sum(pair_sums, axis=1, keepdims=True)
    dense_grad = jnp.sum(jnp.where(route_marks, logit_grad[:, :, None], 0.0), axis=1).astype(BF16)
    input_grad = jnp.dot(dense_grad, router_weight, preferred_element_type=F32).astype(BF16)
    router_part = lax.dot_general(
        dense_grad, inputs, (((0,), (0,)), ((), ())), preferred_element_type=F32
    )
    router_grad = lax.psum(router_part, ("dp", "expert"))
    return (hidden_grad, down_grad, input_grad, router_grad)


INNER = [(1, 2), (2, 1)]
FAR = [(0, 2), (3, 1)]
OUTER = [(0, 1), (3, 2)]
OUTWARD = [(1, 0), (2, 3)]


def plane_swap(x, bits):
    return lax.ppermute(x, "expert", [(i, i ^ bits) for i in range(8)])


def plane_blocks(x, across, along, diagonal):
    return [
        x,
        plane_swap(x, 1),
        across,
        plane_swap(across, 1),
        along,
        plane_swap(along, 1),
        diagonal,
        tuple(plane_swap(piece, 1) for piece in diagonal),
    ]


def plane_diagonal(halves):
    return plane_swap(halves[0], 4), plane_swap(halves[1], 2)


def dense_routes(routes, combine, total_experts):
    marks = make_marks(routes, total_experts)
    counts = jnp.sum(marks.astype(F32), axis=1)
    token_order = jnp.arange(routes.shape[0], dtype=jnp.int32)
    earlier = (token_order[None, :] < token_order[:, None]).astype(BF16)
    before = jnp.dot(earlier, counts.astype(BF16), preferred_element_type=F32)
    routed = counts > 0.0
    weights = jnp.sum(jnp.where(marks, combine[:, :, None], 0.0), axis=1)
    return routed, jnp.where(routed, before, -1.0), weights


def describe(positions, weights):
    high = lax.reduce_precision(weights, 8, 7)
    middle = lax.reduce_precision(weights - high, 8, 7)
    low = weights - high - middle
    stacked = jnp.concatenate([positions, high, middle, low], axis=1)
    return stacked.T.astype(BF16)


def pick_rows(owner, local_experts, total_experts):
    row = lax.broadcasted_iota(jnp.int32, (KINDS * local_experts, LANES), 0)
    column = lax.broadcasted_iota(jnp.int32, (KINDS * local_experts, LANES), 1)
    wanted = (row // local_experts) * total_experts + owner * local_experts + row % local_experts
    return (column == wanted).astype(BF16)


def place_rows(ref, start, width, picker, local_experts, capacity, step, store):
    notes = jnp.dot(
        picker, read_block(ref, start + width, start + width + LANES), preferred_element_type=F32
    )
    slots = lax.broadcasted_iota(jnp.int32, (capacity, LANES), 0).astype(F32)
    marks = []
    scales = []
    for expert in range(local_experts):
        weight = (
            notes[local_experts + expert : local_experts + expert + 1]
            + notes[2 * local_experts + expert : 2 * local_experts + expert + 1]
            + notes[3 * local_experts + expert : 3 * local_experts + expert + 1]
        )
        hit = slots == notes[expert : expert + 1]
        marks.append(jnp.where(hit, 1.0, 0.0).astype(BF16))
        scales.append(jnp.sum(jnp.where(hit, weight, 0.0), axis=1, keepdims=True))
    mark = jnp.concatenate(marks, axis=0)
    scale = jnp.concatenate(scales, axis=0)
    for column in range(0, width, step):
        rows = jnp.dot(
            mark,
            read_block(ref, start + column, start + column + step),
            preferred_element_type=F32,
        )
        rows = (rows * scale).astype(BF16)
        for expert in range(local_experts):
            store(expert, column, step, rows[expert * capacity : (expert + 1) * capacity])


def read_block(block, start, stop):
    if isinstance(block, tuple):
        return jnp.concatenate([half[:, start:stop] for half in block], axis=0)
    return block[:, start:stop]


def split_blocks(blocks):
    flat = []
    for block in blocks:
        flat.extend(block if isinstance(block, tuple) else (block,))
    return flat


def join_blocks(refs, shapes):
    refs = list(refs)
    blocks = []
    for count in shapes:
        blocks.append(refs.pop(0) if count == 1 else (refs.pop(0), refs.pop(0)))
    return blocks


def counts_of(blocks):
    return tuple(2 if isinstance(block, tuple) else 1 for block in blocks)


def hidden_kernel(
    local_experts, total_experts, capacity, width, part, counts, n_after, place, *refs
):
    n_blocks = sum(counts)
    blocks = join_blocks(refs[:n_blocks], counts)
    weight_ref, acts_ref = refs[n_blocks : n_blocks + 2]
    hidden_ref, products_ref, near_ref = refs[n_blocks + 2 + n_after :][:3]
    rows = refs[-1]
    expert = pl.program_id(0)
    me = place[0]

    @pl.when(expert == 0)
    def _():
        picker = pick_rows(me, local_experts, total_experts)
        for k in range(8):
            base = pl.multiple_of((me ^ k) * capacity, 16)

            def store(e, column, step, value, base=base):
                rows[e, pl.ds(base, capacity), column : column + step] = value

            place_rows(blocks[k], 0, width, picker, local_experts, capacity, 512, store)

    hidden = jnp.dot(rows[expert], weight_ref[0], preferred_element_type=F32)
    hidden_ref[0] = hidden.astype(BF16)
    product = hidden * acts_ref[0].astype(F32)
    sums = jnp.sum(product.reshape(8, capacity, product.shape[1]), axis=2)
    empty = jnp.zeros((8, LANES - capacity), F32)
    products_ref[0] = jnp.concatenate([sums, empty], axis=1)
    own = pl.multiple_of(place[1] * part, LANES)
    other = pl.multiple_of(place[2] * part, LANES)
    near_ref[0, :, :part] = rows[expert, :, pl.ds(own, part)]
    near_ref[0, :, part:] = rows[expert, :, pl.ds(other, part)]


def hidden_call(place, blocks, weight, acts, total_experts, capacity, part, after, through):
    local_experts, width, hidden_width = weight.shape
    slots = acts.shape[1]
    kernel = functools.partial(
        hidden_kernel,
        local_experts,
        total_experts,
        capacity,
        width,
        part,
        counts_of(blocks),
        len(after) + len(through),
    )
    flat = split_blocks(blocks)
    tokens = flat[0]
    n_before = 1 + len(flat) + 2 + len(after)
    return pl.pallas_call(
        kernel,
        grid_spec=pltpu.PrefetchScalarGridSpec(
            num_scalar_prefetch=1,
            grid=(local_experts,),
            in_specs=[pl.BlockSpec(b.shape, lambda e, p: (0, 0)) for b in flat]
            + [
                pl.BlockSpec((1, width, hidden_width), lambda e, p: (e, 0, 0)),
                pl.BlockSpec((1, slots, hidden_width), lambda e, p: (e, 0, 0)),
            ]
            + [ANYWHERE] * (len(after) + len(through)),
            out_specs=[
                pl.BlockSpec((1, slots, hidden_width), lambda e, p: (e, 0, 0)),
                pl.BlockSpec((1, 8, LANES), lambda e, p: (e, 0, 0)),
                pl.BlockSpec((1, slots, 2 * part), lambda e, p: (e, 0, 0)),
            ]
            + [ANYWHERE] * len(through),
            scratch_shapes=[pltpu.VMEM((local_experts, slots, width), BF16)],
        ),
        out_shape=[
            jax.ShapeDtypeStruct((local_experts, slots, hidden_width), BF16),
            jax.ShapeDtypeStruct((local_experts, 8, LANES), F32),
            pltpu.VMEM((local_experts, slots, 2 * part), BF16),
        ]
        + [jax.ShapeDtypeStruct(array.shape, array.dtype) for array in through],
        input_output_aliases={n_before + i: 3 + i for i in range(len(through))},
        compiler_params=pltpu.CompilerParams(vmem_limit_bytes=VMEM_LIMIT),
        cost_estimate=pl.CostEstimate(
            flops=2 * local_experts * slots * width * (hidden_width + 256),
            bytes_accessed=2 * (weight.size + 2 * acts.size + 10 * tokens.size),
            transcendentals=0,
        ),
        name="hidden_and_products",
    )(place, *flat, weight, acts, *after, *through)


def rows_kernel(
    local_experts, total_experts, capacity, widths, counts, n_after, place, *refs
):
    n_blocks = sum(counts)
    blocks = join_blocks(refs[:n_blocks], counts)
    beyond, outer = refs[n_blocks + n_after :]
    targets = ((beyond, 0), (beyond, 8 * capacity), (outer, 0))
    me = place[0]
    picker = pick_rows(me, local_experts, total_experts)
    for k in range(8):
        start = 0
        for (out, first), width in zip(targets, widths):
            base = pl.multiple_of(first + (me ^ k) * capacity, 16)

            def store(e, column, step, value, base=base, out=out):
                out[e, pl.ds(base, capacity), column : column + step] = value

            place_rows(blocks[k], start, width, picker, local_experts, capacity, 512, store)
            start += width + LANES


def rows_call(place, blocks, widths, local_experts, total_experts, capacity, after):
    kernel = functools.partial(
        rows_kernel,
        local_experts,
        total_experts,
        capacity,
        widths,
        counts_of(blocks),
        len(after),
    )
    flat = split_blocks(blocks)
    slots = 8 * capacity
    vmem = pl.BlockSpec(memory_space=pltpu.VMEM)
    return pl.pallas_call(
        kernel,
        in_specs=[pl.BlockSpec(memory_space=pltpu.SMEM)]
        + [vmem] * len(flat)
        + [ANYWHERE] * len(after),
        out_specs=[vmem] * 2,
        out_shape=[
            pltpu.VMEM((local_experts, 2 * slots, widths[0]), BF16),
            pltpu.VMEM((local_experts, slots, widths[2]), BF16),
        ],
        compiler_params=pltpu.CompilerParams(vmem_limit_bytes=VMEM_LIMIT),
        cost_estimate=SMALL,
        name="far_rows",
    )(place, *flat, *after)


def copy_kernel(moves, first_target, *refs):
    targets = refs[first_target : first_target + len(moves)]
    for target, pieces in zip(targets, moves):
        for source, source_index, target_index in pieces:
            target[target_index] = refs[source][source_index]


def copies(name, sources, results, moves, after, through=()):
    vmem = pl.BlockSpec(memory_space=pltpu.VMEM)
    n_before = len(sources) + len(after)
    return pl.pallas_call(
        functools.partial(copy_kernel, moves, n_before + len(through)),
        in_specs=[vmem] * len(sources) + [ANYWHERE] * (len(after) + len(through)),
        out_specs=[vmem] * len(results) + [ANYWHERE] * len(through),
        out_shape=[jax.ShapeDtypeStruct(shape, BF16) for shape in results]
        + [jax.ShapeDtypeStruct(array.shape, array.dtype) for array in through],
        input_output_aliases={n_before + i: len(results) + i for i in range(len(through))},
        compiler_params=pltpu.CompilerParams(vmem_limit_bytes=VMEM_LIMIT),
        cost_estimate=SMALL,
        name=name,
    )(*sources, *after, *through)


def rows_of(start, stop):
    return (slice(start, stop), slice(None))


def columns_of(start, stop):
    return (slice(None), slice(start, stop))


def halves_of(across, along, after, through):
    tokens, width = across.shape
    half = tokens // 2
    return copies(
        "token_halves",
        [across, along],
        [(half, width)] * 2,
        [
            [(0, rows_of(0, half), Ellipsis)],
            [(1, rows_of(half, tokens), Ellipsis)],
        ],
        after,
        through,
    )


def outer_product(rows, acts):
    return lax.dot_general(rows, acts, (((0,), (0,)), ((), ())), preferred_element_type=F32)


def down_kernel(near, outer, beyond, near_a, outer_a, inner_a, far_a, *refs):
    own_ref, other_ref = refs[-2:]
    slots = near.shape[1]

    def acts_of(ref):
        return ref[0] if len(ref.shape) == 3 else ref[...]

    total = outer_product(near[0], acts_of(near_a))
    total += outer_product(beyond[0, :slots], acts_of(inner_a))
    total += outer_product(beyond[0, slots:], acts_of(far_a))

    @pl.when(pl.program_id(0) == 0)
    def _():
        other_ref[...] = total.astype(BF16)

    @pl.when(pl.program_id(0) == 1)
    def _():
        own_ref[...] = (total + outer_product(outer[0], acts_of(outer_a))).astype(BF16)


def down_call(expert, near, outer, beyond, acts, after):
    slots = near.shape[1]
    hidden_width = acts[0][0].shape[-1]
    part = outer.shape[2]
    result = pl.BlockSpec((part, hidden_width), lambda i: (0, 0))

    def block_of(array, index):
        if array.ndim == 3:
            return pl.BlockSpec((1, slots, hidden_width), lambda i: (index, 0, 0))
        return pl.BlockSpec((slots, hidden_width), lambda i: (index, 0))

    return pl.pallas_call(
        down_kernel,
        grid=(2,),
        in_specs=[
            pl.BlockSpec((1, slots, part), lambda i: (expert, 0, 1 - i)),
            pl.BlockSpec((1, slots, part), lambda i: (expert, 0, 0)),
            pl.BlockSpec((1, 2 * slots, part), lambda i: (expert, 0, 1 - i)),
        ]
        + [block_of(array, index) for array, index in acts]
        + [ANYWHERE] * len(after),
        out_specs=[result, result],
        out_shape=[jax.ShapeDtypeStruct((part, hidden_width), BF16)] * 2,
        compiler_params=pltpu.CompilerParams(vmem_limit_bytes=VMEM_LIMIT),
        cost_estimate=SMALL,
        name="down_terms",
    )(near, outer, beyond, *[array for array, _ in acts], *after)


def router_kernel(total_experts, n_after, products, places, weights, gate, inputs, *refs):
    input_ref, part_ref = refs[n_after:]
    by_slot = products[...]
    capacity = by_slot.shape[1]
    slots = lax.broadcasted_iota(jnp.int32, (capacity, places.shape[1]), 0).astype(F32)
    sums = []
    for expert in range(total_experts):
        hit = slots == places[expert : expert + 1, :]
        sums.append(
            jnp.sum(jnp.where(hit, by_slot[expert][:, None], 0.0), axis=0, keepdims=True)
        )
    pair_sums = jnp.concatenate(sums, axis=0)
    logits = pair_sums - weights[...] * jnp.sum(pair_sums, axis=0, keepdims=True)
    dense = jnp.where(places[...] >= 0.0, logits, 0.0).astype(BF16)
    step = part_ref.shape[2]
    for index in range(part_ref.shape[0]):
        columns = inputs[:, index * step : (index + 1) * step]
        part_ref[index] = jnp.dot(dense, columns, preferred_element_type=F32)
    input_ref[...] = lax.dot_general(
        dense, gate[...], (((0,), (0,)), ((), ())), preferred_element_type=F32
    ).astype(BF16)


def router_call(products, places, weights, gate, inputs, after):
    vmem = pl.BlockSpec(memory_space=pltpu.VMEM)
    return pl.pallas_call(
        functools.partial(router_kernel, gate.shape[0], len(after)),
        in_specs=[vmem] * 5 + [ANYWHERE] * len(after),
        out_specs=[vmem] * 2,
        out_shape=[
            jax.ShapeDtypeStruct(inputs.shape, BF16),
            jax.ShapeDtypeStruct((8, gate.shape[0], gate.shape[1] // 8), F32),
        ],
        compiler_params=pltpu.CompilerParams(vmem_limit_bytes=VMEM_LIMIT),
        cost_estimate=SMALL,
        name="router_terms",
    )(products, places, weights, gate, inputs, *after)


def sum_kernel(*refs):
    own, first, second, third = refs[:4]
    refs[-1][...] = (own[...] + first[...]) + (second[...] + third[...])


def sum_planes(x, after):
    others = [lax.ppermute(x, "dp", [(i, i ^ k) for i in range(4)]) for k in (1, 2, 3)]
    vmem = pl.BlockSpec(memory_space=pltpu.VMEM)
    return pl.pallas_call(
        sum_kernel,
        in_specs=[vmem] * 4 + [ANYWHERE] * len(after),
        out_specs=vmem,
        out_shape=jax.ShapeDtypeStruct(x.shape, x.dtype),
        cost_estimate=SMALL,
        name="sum_planes",
    )(x, *others, *after)


def local_line(inputs, out_grad, combine, routes, saved_hidden, down_weight, router_weight):
    width = out_grad.shape[1]
    local_experts = down_weight.shape[0]
    total_experts = router_weight.shape[0]
    capacity = saved_hidden.shape[3]
    hidden_width = saved_hidden.shape[4]
    slots = 8 * capacity
    part = width // 4
    plane = lax.axis_index("dp")
    member = lax.axis_index("expert")
    lower = plane < 2
    acts = saved_hidden.reshape(local_experts, slots, hidden_width)

    routed, positions, weights = dense_routes(routes, combine, total_experts)
    notes = describe(positions, weights)
    parts = [out_grad[:, i * part : (i + 1) * part] for i in range(4)]

    pair = jnp.concatenate(
        [jnp.where(lower, parts[2], parts[1]), jnp.where(lower, parts[3], parts[0]), notes], axis=1
    )
    single = jnp.concatenate([jnp.where(lower, parts[1], parts[2]), notes], axis=1)
    from_inner = lax.ppermute(pair, "dp", INNER)
    from_far = lax.ppermute(pair, "dp", FAR)
    from_outer = lax.ppermute(single, "dp", OUTER)

    other_part = jnp.where(lower, 0, 3)
    place = jnp.stack([member, plane, other_part]).astype(jnp.int32)

    tokens = jnp.concatenate([out_grad, notes], axis=1)
    across = plane_swap(tokens, 2)
    along = plane_swap(tokens, 4)
    n_tokens, wide = tokens.shape
    half = n_tokens // 2
    early = local_experts // 2
    *halves, acts_early, acts_late = copies(
        "first_pieces",
        [across, along, acts],
        [(half, wide)] * 2
        + [(early, slots, hidden_width), (local_experts - early, slots, hidden_width)],
        [
            [(0, rows_of(0, half), Ellipsis)],
            [(1, rows_of(half, n_tokens), Ellipsis)],
            [(2, slice(0, early), Ellipsis)],
            [(2, slice(early, local_experts), Ellipsis)],
        ],
        [from_inner, from_far, from_outer],
    )
    diagonal = plane_diagonal(halves)
    own_blocks = plane_blocks(tokens, across, along, diagonal)
    inner_early = lax.ppermute(acts_early, "dp", INNER)
    outer_early = lax.ppermute(acts_early, "dp", OUTER)

    widths = [block.shape[1] for block in (from_inner, from_far, from_outer)]
    starts = [sum(widths[:i]) for i in range(3)]
    (columns,) = copies(
        "side_by_side",
        [from_inner, from_far, from_outer],
        [(n_tokens, sum(widths))],
        [[(i, Ellipsis, columns_of(starts[i], starts[i] + widths[i])) for i in range(3)]],
        diagonal,
    )
    columns_across = plane_swap(columns, 2)
    columns_along = plane_swap(columns, 4)

    hidden, products, near, acts_late = hidden_call(
        place, own_blocks, down_weight, acts, total_experts, capacity, part, [columns],
        [acts_late],
    )
    outer_late = lax.ppermute(acts_late, "dp", OUTER)

    *column_halves, outer_early = halves_of(
        columns_across, columns_along, [hidden, inner_early], [outer_early]
    )
    far_early = lax.ppermute(outer_early, "dp", INNER)
    other_blocks = plane_blocks(
        columns, columns_across, columns_along, plane_diagonal(column_halves)
    )
    returned = lax.all_to_all(
        products.transpose(1, 0, 2), "expert", split_axis=0, concat_axis=0
    ).reshape(total_experts, LANES)
    beyond, outer = rows_call(
        place, other_blocks, (2 * part, 2 * part, part), local_experts, total_experts, capacity,
        [returned],
    )

    cut = hidden_width // 2
    chunks = [(2, 0, hidden_width), (3, 0, cut), (3, cut, hidden_width)]
    homes = copies(
        "home_acts",
        [acts_late, outer_late],
        [(2 * slots, stop - start) for _, start, stop in chunks],
        [
            [
                (source, (expert - early, slice(None), slice(start, stop)), rows_of(source * slots, (source + 1) * slots))
                for source in range(2)
            ]
            for expert, start, stop in chunks
        ],
        [outer, far_early],
    )
    beyonds = [lax.ppermute(home, "dp", INNER) for home in homes]

    def down(expert, pieces, after):
        own, other = down_call(expert, near, outer, beyond, pieces, after)
        return own, lax.ppermute(other, "dp", OUTWARD)

    downs = []
    for expert in range(early):
        pieces = [(a, expert) for a in (acts_early, outer_early, inner_early, far_early)]
        downs.append(down(expert, pieces, list(homes) + [own for own, _ in downs]))
    input_grad, router_part = router_call(
        returned, positions.T, weights.T, router_weight, inputs, [downs[-1][0]]
    )
    reduced = jnp.sum(
        lax.all_to_all(router_part, "expert", split_axis=0, concat_axis=0), axis=0
    )
    for index, (expert, start, stop) in enumerate(chunks):
        pieces = [(homes[index], 0), (homes[index], 1), (beyonds[index], 0), (beyonds[index], 1)]
        downs.append(down(expert, pieces, [downs[-1][0], downs[-2][1], reduced]))
    summed = sum_planes(reduced, [downs[-1][0]])
    router_grad = (
        lax.all_gather(summed, "expert").transpose(1, 0, 2).reshape(total_experts, width)
    )

    finished = [(own.astype(F32) + came.astype(F32)).astype(BF16) for own, came in downs]
    down_grad = jnp.stack(finished[:3] + [jnp.concatenate(finished[3:], axis=1)])

    hidden_grad = hidden.reshape(saved_hidden.shape)
    return (hidden_grad, down_grad, input_grad, router_grad)


def solution(mesh):
    in_line = mesh.shape["dp"] == 4 and mesh.shape["expert"] == 8

    def local(inputs, out_grad, combine, routes, saved_hidden, down_weight, router_weight):
        tokens, width = out_grad.shape
        fits = (
            in_line
            and tokens == LANES
            and KINDS * router_weight.shape[0] == LANES
            and width % 2048 == 0
            and saved_hidden.shape[3] % 16 == 0
            and saved_hidden.shape[4] % LANES == 0
        )
        body = local_line if fits else local_any
        return body(
            inputs, out_grad, combine, routes, saved_hidden, down_weight, router_weight
        )

    placed = (
        P(("dp", "expert"), None),
        P(("dp", "expert"), None),
        P(("dp", "expert"), None),
        P(("dp", "expert"), None),
        P("dp", "expert", None, None, None),
        P("expert", None, None),
        P(),
    )
    return jax.shard_map(
        local,
        mesh=mesh,
        in_specs=placed,
        out_specs=(
            P("dp", "expert", None, None, None),
            P("expert", "dp", None),
            P(("dp", "expert"), None),
            P(),
        ),
        check_vma=False,
    )
```

```python
import functools

import jax
import jax.numpy as jnp
from jax import lax
from jax.experimental import pallas as pl
from jax.experimental.pallas import tpu as pltpu
from jax.sharding import PartitionSpec as P

F32 = jnp.float32
BF16 = jnp.bfloat16
LANES = 128
KINDS = 4
MIB = 1024 * 1024
VMEM_LIMIT = 51 * MIB
ANYWHERE = pl.BlockSpec(memory_space=pl.ANY)
SMALL = pl.CostEstimate(flops=1000, bytes_accessed=1000, transcendentals=0)


def make_marks(block_routes, total_experts):
    return block_routes[:, :, None] == jnp.arange(total_experts, dtype=jnp.int32)[None, None, :]


def slot_positions(route_marks):
    counts = jnp.sum(route_marks.astype(BF16), axis=1)
    token_order = jnp.arange(route_marks.shape[0], dtype=jnp.int32)
    earlier = (token_order[None, :] < token_order[:, None]).astype(BF16)
    before = jnp.dot(earlier, counts, preferred_element_type=F32)
    picked = jnp.sum(jnp.where(route_marks, before[:, None, :], 0.0), axis=2)
    return picked.astype(jnp.int32)


def pack_rows(scaled, lane_index, owner_slot, positions, local_experts, groups, capacity):
    width = scaled.shape[-1]
    flat_index = (owner_slot * groups + lane_index) * capacity + positions
    zero_rows = jnp.zeros((local_experts * groups * capacity, width), BF16)
    filled = zero_rows.at[flat_index.reshape(-1)].set(scaled.reshape(-1, width))
    return filled.reshape(local_experts, groups, capacity, width)


def local_any(inputs, out_grad, combine, routes, saved_hidden, down_weight, router_weight):
    token_count, width = out_grad.shape
    local_experts = down_weight.shape[0]
    total_experts = router_weight.shape[0]
    groups = lax.axis_size("expert")
    capacity = saved_hidden.shape[3]
    hidden_width = saved_hidden.shape[4]
    route_marks = make_marks(routes, total_experts)
    positions = slot_positions(route_marks)
    owner_dev = routes // local_experts
    owner_slot = routes % local_experts
    scaled = (combine[:, :, None] * out_grad[:, None, :].astype(F32)).astype(BF16)
    packed = pack_rows(scaled, owner_dev, owner_slot, positions, local_experts, groups, capacity)
    received = lax.all_to_all(packed, "expert", split_axis=1, concat_axis=1, tiled=True)
    hidden_local = saved_hidden[0]
    products_list = []
    hidden_list = []
    weight_terms = []
    for expert in range(local_experts):
        slot_rows = received[expert].reshape(groups * capacity, width)
        slot_acts = hidden_local[expert].reshape(groups * capacity, hidden_width)
        weight = down_weight[expert]
        hidden = jnp.dot(slot_rows, weight, preferred_element_type=F32)
        products_list.append(jnp.sum(hidden * slot_acts.astype(F32), axis=1))
        hidden_list.append(hidden.astype(BF16))
        weight_terms.append(
            lax.dot_general(
                slot_rows, slot_acts, (((0,), (0,)), ((), ())), preferred_element_type=F32
            )
        )
    down_grad = lax.psum_scatter(
        jnp.stack(weight_terms).astype(BF16), "dp", scatter_dimension=1, tiled=True
    )
    hidden_grad = jnp.stack(hidden_list).reshape(1, local_experts, groups, capacity, hidden_width)
    slot_products = jnp.stack(products_list).reshape(local_experts, groups, capacity)
    returned = lax.all_to_all(slot_products, "expert", split_axis=1, concat_axis=1, tiled=True)
    pair_index = (owner_slot * groups + owner_dev) * capacity + positions
    pair_sums = returned.reshape(-1)[pair_index]
    logit_grad = pair_sums - combine * jnp.sum(pair_sums, axis=1, keepdims=True)
    dense_grad = jnp.sum(jnp.where(route_marks, logit_grad[:, :, None], 0.0), axis=1).astype(BF16)
    input_grad = jnp.dot(dense_grad, router_weight, preferred_element_type=F32).astype(BF16)
    router_part = lax.dot_general(
        dense_grad, inputs, (((0,), (0,)), ((), ())), preferred_element_type=F32
    )
    router_grad = lax.psum(router_part, ("dp", "expert"))
    return (hidden_grad, down_grad, input_grad, router_grad)


INNER = [(1, 2), (2, 1)]
FAR = [(0, 2), (3, 1)]
OUTER = [(0, 1), (3, 2)]
OUTWARD = [(1, 0), (2, 3)]


def plane_swap(x, bits):
    return lax.ppermute(x, "expert", [(i, i ^ bits) for i in range(8)])


def plane_blocks(x, across, along, stacked, diagonal):
    swapped = plane_swap(stacked, 1)
    corner = [plane_swap(piece, 1) for piece in diagonal]
    return [
        [(x, None)],
        [(swapped, 0)],
        [(across, None)],
        [(swapped, 1)],
        [(along, None)],
        [(swapped, 2)],
        [(piece, None) for piece in diagonal],
        [(piece, None) for piece in corner],
    ]


def plane_diagonal(halves):
    return plane_swap(halves[0], 4), plane_swap(halves[1], 2)


def dense_routes(routes, combine, total_experts):
    marks = make_marks(routes, total_experts)
    counts = jnp.sum(marks.astype(F32), axis=1)
    token_order = jnp.arange(routes.shape[0], dtype=jnp.int32)
    earlier = (token_order[None, :] < token_order[:, None]).astype(BF16)
    before = jnp.dot(earlier, counts.astype(BF16), preferred_element_type=F32)
    routed = counts > 0.0
    weights = jnp.sum(jnp.where(marks, combine[:, :, None], 0.0), axis=1)
    return routed, jnp.where(routed, before, -1.0), weights


def describe(positions, weights):
    high = lax.reduce_precision(weights, 8, 7)
    middle = lax.reduce_precision(weights - high, 8, 7)
    low = weights - high - middle
    stacked = jnp.concatenate([positions, high, middle, low], axis=1)
    return stacked.T.astype(BF16)


def pick_rows(owner, local_experts, total_experts):
    row = lax.broadcasted_iota(jnp.int32, (KINDS * local_experts, LANES), 0)
    column = lax.broadcasted_iota(jnp.int32, (KINDS * local_experts, LANES), 1)
    wanted = (row // local_experts) * total_experts + owner * local_experts + row % local_experts
    return (column == wanted).astype(BF16)


def place_rows(ref, start, width, picker, local_experts, capacity, step, store):
    notes = jnp.dot(
        picker, read_block(ref, start + width, start + width + LANES), preferred_element_type=F32
    )
    slots = lax.broadcasted_iota(jnp.int32, (capacity, LANES), 0).astype(F32)
    marks = []
    scales = []
    for expert in range(local_experts):
        weight = (
            notes[local_experts + expert : local_experts + expert + 1]
            + notes[2 * local_experts + expert : 2 * local_experts + expert + 1]
            + notes[3 * local_experts + expert : 3 * local_experts + expert + 1]
        )
        hit = slots == notes[expert : expert + 1]
        marks.append(jnp.where(hit, 1.0, 0.0).astype(BF16))
        scales.append(jnp.sum(jnp.where(hit, weight, 0.0), axis=1, keepdims=True))
    mark = jnp.concatenate(marks, axis=0)
    scale = jnp.concatenate(scales, axis=0)
    for column in range(0, width, step):
        rows = jnp.dot(
            mark,
            read_block(ref, start + column, start + column + step),
            preferred_element_type=F32,
        )
        rows = (rows * scale).astype(BF16)
        for expert in range(local_experts):
            store(expert, column, step, rows[expert * capacity : (expert + 1) * capacity])


def read_block(block, start, stop):
    pieces = []
    for ref, index in block:
        pieces.append(ref[:, start:stop] if index is None else ref[index, :, start:stop])
    return jnp.concatenate(pieces, axis=0) if len(pieces) > 1 else pieces[0]


def arrays_of(blocks):
    arrays = []
    layout = []
    for block in blocks:
        pieces = []
        for array, index in block:
            found = [i for i, known in enumerate(arrays) if known is array]
            if not found:
                arrays.append(array)
                found = [len(arrays) - 1]
            pieces.append((found[0], index))
        layout.append(pieces)
    return arrays, layout


def blocks_of(refs, layout):
    return [[(refs[place], index) for place, index in pieces] for pieces in layout]


def hidden_kernel(
    local_experts, total_experts, capacity, width, part, n_blocks, layout, n_after, place, *refs
):
    blocks = blocks_of(refs[:n_blocks], layout)
    weight_ref, acts_ref = refs[n_blocks : n_blocks + 2]
    hidden_ref, products_ref, near_ref = refs[n_blocks + 2 + n_after :][:3]
    rows = refs[-1]
    expert = pl.program_id(0)
    me = place[0]

    @pl.when(expert == 0)
    def _():
        picker = pick_rows(me, local_experts, total_experts)
        for k in range(8):
            base = pl.multiple_of((me ^ k) * capacity, 16)

            def store(e, column, step, value, base=base):
                rows[e, pl.ds(base, capacity), column : column + step] = value

            place_rows(blocks[k], 0, width, picker, local_experts, capacity, 512, store)

    hidden = jnp.dot(rows[expert], weight_ref[0], preferred_element_type=F32)
    hidden_ref[0] = hidden.astype(BF16)
    product = hidden * acts_ref[0].astype(F32)
    sums = jnp.sum(product.reshape(8, capacity, product.shape[1]), axis=2)
    empty = jnp.zeros((8, LANES - capacity), F32)
    products_ref[0] = jnp.concatenate([sums, empty], axis=1)
    own = pl.multiple_of(place[1] * part, LANES)
    other = pl.multiple_of(place[2] * part, LANES)
    near_ref[0, :, :part] = rows[expert, :, pl.ds(own, part)]
    near_ref[0, :, part:] = rows[expert, :, pl.ds(other, part)]


def whole_block(shape):
    return pl.BlockSpec(shape, lambda *_: (0,) * len(shape))


def hidden_call(place, blocks, weight, acts, total_experts, capacity, part, after, through):
    local_experts, width, hidden_width = weight.shape
    slots = acts.shape[1]
    flat, layout = arrays_of(blocks)
    kernel = functools.partial(
        hidden_kernel,
        local_experts,
        total_experts,
        capacity,
        width,
        part,
        len(flat),
        layout,
        len(after) + len(through),
    )
    tokens = flat[0]
    n_before = 1 + len(flat) + 2 + len(after)
    return pl.pallas_call(
        kernel,
        grid_spec=pltpu.PrefetchScalarGridSpec(
            num_scalar_prefetch=1,
            grid=(local_experts,),
            in_specs=[whole_block(b.shape) for b in flat]
            + [
                pl.BlockSpec((1, width, hidden_width), lambda e, p: (e, 0, 0)),
                pl.BlockSpec((1, slots, hidden_width), lambda e, p: (e, 0, 0)),
            ]
            + [ANYWHERE] * (len(after) + len(through)),
            out_specs=[
                pl.BlockSpec((1, slots, hidden_width), lambda e, p: (e, 0, 0)),
                pl.BlockSpec((1, 8, LANES), lambda e, p: (e, 0, 0)),
                pl.BlockSpec((1, slots, 2 * part), lambda e, p: (e, 0, 0)),
            ]
            + [ANYWHERE] * len(through),
            scratch_shapes=[pltpu.VMEM((local_experts, slots, width), BF16)],
        ),
        out_shape=[
            jax.ShapeDtypeStruct((local_experts, slots, hidden_width), BF16),
            jax.ShapeDtypeStruct((local_experts, 8, LANES), F32),
            jax.ShapeDtypeStruct((local_experts, slots, 2 * part), BF16),
        ]
        + [jax.ShapeDtypeStruct(array.shape, array.dtype) for array in through],
        input_output_aliases={n_before + i: 3 + i for i in range(len(through))},
        compiler_params=pltpu.CompilerParams(vmem_limit_bytes=56 * MIB),
        cost_estimate=pl.CostEstimate(
            flops=2 * local_experts * slots * width * (hidden_width + 256),
            bytes_accessed=2 * (weight.size + 2 * acts.size + 10 * tokens.size),
            transcendentals=0,
        ),
        name="hidden_and_products",
    )(place, *flat, weight, acts, *after, *through)


def rows_kernel(
    local_experts, total_experts, capacity, widths, n_blocks, layout, n_after, place, *refs
):
    blocks = blocks_of(refs[:n_blocks], layout)
    outs = refs[n_blocks + n_after : n_blocks + n_after + local_experts]
    rows, stored = refs[n_blocks + n_after + local_experts :]
    slots = 8 * capacity
    me = place[0]
    picker = pick_rows(me, local_experts, total_experts)
    start = 0
    stores = []
    for index, width in enumerate(widths):
        for k in range(8):
            base = pl.multiple_of(index * slots + (me ^ k) * capacity, 16)

            def store(e, column, step, value, base=base):
                rows[e, pl.ds(base, capacity), column : column + step] = value

            place_rows(blocks[k], start, width, picker, local_experts, capacity, 512, store)
        start += width + LANES
        group = pl.ds(index * slots, slots)
        for expert in range(local_experts):
            held = rows.at[expert, group]
            target = outs[expert].at[group]
            stores.append(pltpu.make_async_copy(held, target, stored.at[index, expert]))
            stores[-1].start()
    for copy in stores:
        copy.wait()


def rows_call(place, blocks, widths, local_experts, total_experts, capacity, after):
    flat, layout = arrays_of(blocks)
    shape = (len(widths) * 8 * capacity, widths[0])
    kernel = functools.partial(
        rows_kernel,
        local_experts,
        total_experts,
        capacity,
        widths,
        len(flat),
        layout,
        len(after),
    )
    return pl.pallas_call(
        kernel,
        in_specs=[pl.BlockSpec(memory_space=pltpu.SMEM)]
        + [pl.BlockSpec(memory_space=pltpu.VMEM)] * len(flat)
        + [ANYWHERE] * len(after),
        out_specs=[pl.BlockSpec(memory_space=pltpu.VMEM)] + [ANYWHERE] * (local_experts - 1),
        out_shape=[pltpu.VMEM(shape, BF16)]
        + [jax.ShapeDtypeStruct(shape, BF16)] * (local_experts - 1),
        scratch_shapes=[
            pltpu.VMEM((local_experts, *shape), BF16),
            pltpu.SemaphoreType.DMA((len(widths), local_experts)),
        ],
        compiler_params=pltpu.CompilerParams(vmem_limit_bytes=56 * MIB),
        cost_estimate=pl.CostEstimate(
            flops=2 * local_experts * 8 * capacity * 256 * sum(widths),
            bytes_accessed=2 * local_experts * shape[0] * shape[1],
            transcendentals=0,
        ),
        name="far_rows",
    )(place, *flat, *after)


def copy_kernel(moves, first_target, *refs):
    targets = refs[first_target : first_target + len(moves)]
    for target, pieces in zip(targets, moves):
        for source, source_index, target_index in pieces:
            target[target_index] = refs[source][source_index]


def copies(name, sources, results, moves, after, vmem_limit):
    vmem = pl.BlockSpec(memory_space=pltpu.VMEM)
    return pl.pallas_call(
        functools.partial(copy_kernel, moves, len(sources) + len(after)),
        in_specs=[vmem] * len(sources) + [ANYWHERE] * len(after),
        out_specs=[vmem] * len(results),
        out_shape=[jax.ShapeDtypeStruct(shape, BF16) for shape in results],
        compiler_params=pltpu.CompilerParams(vmem_limit_bytes=vmem_limit),
        cost_estimate=pl.CostEstimate(
            flops=0,
            bytes_accessed=4 * sum(array.size for array in sources),
            transcendentals=0,
        ),
        name=name,
    )(*sources, *after)


def nothing_kernel(*_):
    pass


def held_until(arrays, after):
    return pl.pallas_call(
        nothing_kernel,
        in_specs=[ANYWHERE] * (len(arrays) + len(after)),
        out_specs=[ANYWHERE] * len(arrays),
        out_shape=[jax.ShapeDtypeStruct(array.shape, array.dtype) for array in arrays],
        input_output_aliases={i: i for i in range(len(arrays))},
        compiler_params=pltpu.CompilerParams(has_side_effects=True),
        cost_estimate=SMALL,
        name="held_until",
    )(*arrays, *after)


def rows_of(start, stop):
    return (slice(start, stop), slice(None))


def columns_of(start, stop):
    return (slice(None), slice(start, stop))


def outer_product(rows, acts):
    return lax.dot_general(rows, acts, (((0,), (0,)), ((), ())), preferred_element_type=F32)


def down_kernel(places, n_after, rows, *refs):
    sources = refs[:5]
    own_ref, other_ref, near, acts, results, loaded, stored = refs[5 + n_after :]
    slots, width = near.shape
    part = width // 2
    targets = [near] + [acts.at[pl.ds(i * slots, slots)] for i in range(4)]
    loads = [
        pltpu.make_async_copy(source.at[place], target, loaded.at[i])
        for i, (source, place, target) in enumerate(zip(sources, places, targets))
    ]
    for load in loads:
        load.start()
    stores = [
        pltpu.make_async_copy(results.at[i], target, stored.at[i])
        for i, target in enumerate((other_ref, own_ref))
    ]
    for load in loads[:4]:
        load.wait()
    total = outer_product(near[:, part:], acts[:slots])
    total += outer_product(rows[: 2 * slots, part:], acts[slots : 3 * slots])
    results[0] = total.astype(BF16)
    stores[0].start()
    loads[4].wait()
    total = outer_product(near[:, :part], acts[:slots])
    total += outer_product(rows[:, :part], acts[slots:])
    results[1] = total.astype(BF16)
    stores[1].start()
    for store in stores:
        store.wait()


def down_call(rows, near, acts, after):
    sources = [near, *acts]
    arrays = [array for array, _ in sources]
    places = [place for _, place in sources]
    slots, hidden_width = arrays[1].shape[1:]
    width = rows.shape[1]
    return pl.pallas_call(
        functools.partial(down_kernel, places, len(after)),
        in_specs=[pl.BlockSpec(memory_space=pltpu.VMEM)]
        + [ANYWHERE] * (len(arrays) + len(after)),
        out_specs=[ANYWHERE] * 2,
        out_shape=[jax.ShapeDtypeStruct((width // 2, hidden_width), BF16)] * 2,
        scratch_shapes=[
            pltpu.VMEM((slots, width), BF16),
            pltpu.VMEM((4 * slots, hidden_width), BF16),
            pltpu.VMEM((2, width // 2, hidden_width), BF16),
            pltpu.SemaphoreType.DMA((5,)),
            pltpu.SemaphoreType.DMA((2,)),
        ],
        compiler_params=pltpu.CompilerParams(vmem_limit_bytes=50 * MIB),
        cost_estimate=SMALL,
        name="down_terms",
    )(pltpu.with_memory_space_constraint(rows, pltpu.VMEM), *arrays, *after)


def router_kernel(total_experts, n_after, products, places, weights, gate, inputs, *refs):
    input_ref, part_ref = refs[n_after:]
    by_slot = products[...]
    capacity = by_slot.shape[1]
    slots = lax.broadcasted_iota(jnp.int32, (capacity, places.shape[1]), 0).astype(F32)
    sums = []
    for expert in range(total_experts):
        hit = slots == places[expert : expert + 1, :]
        sums.append(
            jnp.sum(jnp.where(hit, by_slot[expert][:, None], 0.0), axis=0, keepdims=True)
        )
    pair_sums = jnp.concatenate(sums, axis=0)
    logits = pair_sums - weights[...] * jnp.sum(pair_sums, axis=0, keepdims=True)
    dense = jnp.where(places[...] >= 0.0, logits, 0.0).astype(BF16)
    step = part_ref.shape[2]
    for index in range(part_ref.shape[0]):
        columns = inputs[:, index * step : (index + 1) * step]
        part_ref[index] = jnp.dot(dense, columns, preferred_element_type=F32)
    input_ref[...] = lax.dot_general(
        dense, gate[...], (((0,), (0,)), ((), ())), preferred_element_type=F32
    ).astype(BF16)


def router_call(products, places, weights, gate, inputs, after):
    vmem = pl.BlockSpec(memory_space=pltpu.VMEM)
    return pl.pallas_call(
        functools.partial(router_kernel, gate.shape[0], len(after)),
        in_specs=[vmem] * 5 + [ANYWHERE] * len(after),
        out_specs=[vmem] * 2,
        out_shape=[
            jax.ShapeDtypeStruct(inputs.shape, BF16),
            jax.ShapeDtypeStruct((8, gate.shape[0], gate.shape[1] // 8), F32),
        ],
        compiler_params=pltpu.CompilerParams(vmem_limit_bytes=24 * MIB),
        cost_estimate=SMALL,
        name="router_terms",
    )(products, places, weights, gate, inputs, *after)


def sum_kernel(*refs):
    own, first, second, third = refs[:4]
    refs[-1][...] = (own[...] + first[...]) + (second[...] + third[...])


def sum_planes(x, others, after):
    vmem = pl.BlockSpec(memory_space=pltpu.VMEM)
    return pl.pallas_call(
        sum_kernel,
        in_specs=[vmem] * 4 + [ANYWHERE] * len(after),
        out_specs=vmem,
        out_shape=jax.ShapeDtypeStruct(x.shape, x.dtype),
        cost_estimate=SMALL,
        name="sum_planes",
    )(x, *others, *after)


def local_line(inputs, out_grad, combine, routes, saved_hidden, down_weight, router_weight):
    width = out_grad.shape[1]
    local_experts = down_weight.shape[0]
    total_experts = router_weight.shape[0]
    capacity = saved_hidden.shape[3]
    hidden_width = saved_hidden.shape[4]
    slots = 8 * capacity
    part = width // 4
    plane = lax.axis_index("dp")
    member = lax.axis_index("expert")
    lower = plane < 2
    acts = saved_hidden.reshape(local_experts, slots, hidden_width)

    routed, positions, weights = dense_routes(routes, combine, total_experts)
    notes = describe(positions, weights)
    parts = [out_grad[:, i * part : (i + 1) * part] for i in range(4)]

    pair = jnp.concatenate(
        [jnp.where(lower, parts[2], parts[1]), jnp.where(lower, parts[3], parts[0]), notes], axis=1
    )
    single = jnp.concatenate([jnp.where(lower, parts[1], parts[2]), notes], axis=1)
    from_inner = lax.ppermute(pair, "dp", INNER)
    from_far = lax.ppermute(pair, "dp", FAR)
    from_outer = lax.ppermute(single, "dp", OUTER)

    other_part = jnp.where(lower, 0, 3)
    place = jnp.stack([member, plane, other_part]).astype(jnp.int32)

    tokens = jnp.concatenate([out_grad, notes], axis=1)
    across = plane_swap(tokens, 2)
    along = plane_swap(tokens, 4)
    n_tokens = tokens.shape[0]
    half = n_tokens // 2

    groups = [(0, 2), (2, local_experts)]
    acts_early, *acts_late = copies(
        "acts_pieces",
        [acts],
        [(stop - start, slots, hidden_width) for start, stop in groups],
        [[(0, slice(start, stop), Ellipsis)] for start, stop in groups],
        [across],
        60 * MIB,
    )
    *halves, stacked = copies(
        "first_pieces",
        [across, along, tokens],
        [(half, tokens.shape[1])] * 2 + [(3, *tokens.shape)],
        [[(0, rows_of(0, half), Ellipsis)], [(1, rows_of(half, n_tokens), Ellipsis)]]
        + [[(source, Ellipsis, index) for index, source in enumerate((2, 0, 1))]],
        [from_inner, from_far, from_outer, acts_early],
        60 * MIB,
    )
    diagonal = plane_diagonal(halves)
    own_blocks = plane_blocks(tokens, across, along, stacked, diagonal)
    inners = [lax.ppermute(acts_early, "dp", INNER)]
    outers = [lax.ppermute(acts_early, "dp", OUTER)]

    widths = [block.shape[1] for block in (from_inner, from_far, from_outer)]
    starts = [sum(widths[:i]) for i in range(3)]
    (columns,) = copies(
        "side_by_side",
        [from_inner, from_far, from_outer],
        [(n_tokens, sum(widths))],
        [[(i, Ellipsis, columns_of(starts[i], starts[i] + widths[i])) for i in range(3)]],
        diagonal,
        60 * MIB,
    )
    columns_across = plane_swap(columns, 2)
    columns_along = plane_swap(columns, 4)

    hidden, products, near, *late = hidden_call(
        place, own_blocks, down_weight, acts, total_experts, capacity, part,
        [columns], acts_late,
    )
    inners += [lax.ppermute(a, "dp", INNER) for a in late]
    outers += [lax.ppermute(a, "dp", OUTER) for a in late]
    fars = [lax.ppermute(outers[0], "dp", INNER)]
    fars += [
        lax.ppermute(outers[1][i : i + 1], "dp", INNER) for i in range(local_experts - 2)
    ]

    *column_halves, stacked = copies(
        "second_pieces",
        [columns_across, columns_along, columns],
        [(half, sum(widths))] * 2 + [(3, *columns.shape)],
        [[(0, rows_of(0, half), Ellipsis)], [(1, rows_of(half, n_tokens), Ellipsis)]]
        + [[(source, Ellipsis, index) for index, source in enumerate((2, 0, 1))]],
        [hidden, outers[0], inners[0]],
        56 * MIB,
    )
    other_blocks = plane_blocks(
        columns, columns_across, columns_along, stacked, plane_diagonal(column_halves)
    )
    rows = rows_call(
        place, other_blocks, (2 * part, 2 * part, part), local_experts, total_experts, capacity, []
    )

    def down(expert, after, hold=()):
        group, place = divmod(expert, 2)
        far = (fars[0], expert) if expert < 2 else (fars[expert - 1], 0)
        pieces = [(acts, expert), (inners[group], place), far, (outers[group], place)]
        own, other = down_call(rows[expert], (near, expert), pieces, after)
        if hold:
            (other,) = held_until([other], hold)
        return own, lax.ppermute(other, "dp", OUTWARD)

    def finish(own, came):
        return (own.astype(F32) + came.astype(F32)).astype(BF16)

    downs = [down(0, [])]
    downs.append(down(1, [downs[0][0]]))
    returned = lax.all_to_all(
        products.transpose(1, 0, 2), "expert", split_axis=0, concat_axis=0
    ).reshape(total_experts, LANES)
    input_grad, router_part = router_call(
        returned, positions.T, weights.T, router_weight, inputs, [downs[1][0]]
    )
    downs.append(down(2, [downs[1][0], inners[1], downs[0][1]]))
    (router_part,) = held_until([router_part], [downs[2][0]])
    reduced = jnp.sum(
        lax.all_to_all(router_part, "expert", split_axis=0, concat_axis=0), axis=0
    )
    others = [lax.ppermute(reduced, "dp", [(i, i ^ k) for i in range(4)]) for k in (1, 2, 3)]
    finished = [finish(*downs[0])]
    downs.append(down(3, [reduced, *finished], others))
    finished += [finish(*downs[expert]) for expert in range(1, 4)]
    summed = sum_planes(reduced, others, [downs[-1][0]])
    router_grad = (
        lax.all_gather(summed, "expert").transpose(1, 0, 2).reshape(total_experts, width)
    )

    down_grad = jnp.stack(finished)

    hidden_grad = hidden.reshape(saved_hidden.shape)
    return (hidden_grad, down_grad, input_grad, router_grad)


def solution(mesh):
    in_line = mesh.shape["dp"] == 4 and mesh.shape["expert"] == 8

    def local(inputs, out_grad, combine, routes, saved_hidden, down_weight, router_weight):
        tokens, width = out_grad.shape
        fits = (
            in_line
            and tokens == LANES
            and KINDS * router_weight.shape[0] == LANES
            and width % 2048 == 0
            and saved_hidden.shape[3] % 16 == 0
            and saved_hidden.shape[4] % LANES == 0
        )
        body = local_line if fits else local_any
        return body(
            inputs, out_grad, combine, routes, saved_hidden, down_weight, router_weight
        )

    placed = (
        P(("dp", "expert"), None),
        P(("dp", "expert"), None),
        P(("dp", "expert"), None),
        P(("dp", "expert"), None),
        P("dp", "expert", None, None, None),
        P("expert", None, None),
        P(),
    )
    return jax.shard_map(
        local,
        mesh=mesh,
        in_specs=placed,
        out_specs=(
            P("dp", "expert", None, None, None),
            P("expert", "dp", None),
            P(("dp", "expert"), None),
            P(),
        ),
        check_vma=False,
    )
```

```python
import functools

import jax
import jax.numpy as jnp
from jax import lax
from jax.experimental import pallas as pl
from jax.experimental.pallas import tpu as pltpu
from jax.sharding import PartitionSpec as P

F32 = jnp.float32
BF16 = jnp.bfloat16
LANES = 128
KINDS = 4
MIB = 1024 * 1024
VMEM_LIMIT = 51 * MIB
ANYWHERE = pl.BlockSpec(memory_space=pl.ANY)
SMALL = pl.CostEstimate(flops=1000, bytes_accessed=1000, transcendentals=0)


def make_marks(block_routes, total_experts):
    return block_routes[:, :, None] == jnp.arange(total_experts, dtype=jnp.int32)[None, None, :]


def slot_positions(route_marks):
    counts = jnp.sum(route_marks.astype(BF16), axis=1)
    token_order = jnp.arange(route_marks.shape[0], dtype=jnp.int32)
    earlier = (token_order[None, :] < token_order[:, None]).astype(BF16)
    before = jnp.dot(earlier, counts, preferred_element_type=F32)
    picked = jnp.sum(jnp.where(route_marks, before[:, None, :], 0.0), axis=2)
    return picked.astype(jnp.int32)


def pack_rows(scaled, lane_index, owner_slot, positions, local_experts, groups, capacity):
    width = scaled.shape[-1]
    flat_index = (owner_slot * groups + lane_index) * capacity + positions
    zero_rows = jnp.zeros((local_experts * groups * capacity, width), BF16)
    filled = zero_rows.at[flat_index.reshape(-1)].set(scaled.reshape(-1, width))
    return filled.reshape(local_experts, groups, capacity, width)


def local_any(inputs, out_grad, combine, routes, saved_hidden, down_weight, router_weight):
    token_count, width = out_grad.shape
    local_experts = down_weight.shape[0]
    total_experts = router_weight.shape[0]
    groups = lax.axis_size("expert")
    capacity = saved_hidden.shape[3]
    hidden_width = saved_hidden.shape[4]
    route_marks = make_marks(routes, total_experts)
    positions = slot_positions(route_marks)
    owner_dev = routes // local_experts
    owner_slot = routes % local_experts
    scaled = (combine[:, :, None] * out_grad[:, None, :].astype(F32)).astype(BF16)
    packed = pack_rows(scaled, owner_dev, owner_slot, positions, local_experts, groups, capacity)
    received = lax.all_to_all(packed, "expert", split_axis=1, concat_axis=1, tiled=True)
    hidden_local = saved_hidden[0]
    products_list = []
    hidden_list = []
    weight_terms = []
    for expert in range(local_experts):
        slot_rows = received[expert].reshape(groups * capacity, width)
        slot_acts = hidden_local[expert].reshape(groups * capacity, hidden_width)
        weight = down_weight[expert]
        hidden = jnp.dot(slot_rows, weight, preferred_element_type=F32)
        products_list.append(jnp.sum(hidden * slot_acts.astype(F32), axis=1))
        hidden_list.append(hidden.astype(BF16))
        weight_terms.append(
            lax.dot_general(
                slot_rows, slot_acts, (((0,), (0,)), ((), ())), preferred_element_type=F32
            )
        )
    down_grad = lax.psum_scatter(
        jnp.stack(weight_terms).astype(BF16), "dp", scatter_dimension=1, tiled=True
    )
    hidden_grad = jnp.stack(hidden_list).reshape(1, local_experts, groups, capacity, hidden_width)
    slot_products = jnp.stack(products_list).reshape(local_experts, groups, capacity)
    returned = lax.all_to_all(slot_products, "expert", split_axis=1, concat_axis=1, tiled=True)
    pair_index = (owner_slot * groups + owner_dev) * capacity + positions
    pair_sums = returned.reshape(-1)[pair_index]
    logit_grad = pair_sums - combine * jnp.sum(pair_sums, axis=1, keepdims=True)
    dense_grad = jnp.sum(jnp.where(route_marks, logit_grad[:, :, None], 0.0), axis=1).astype(BF16)
    input_grad = jnp.dot(dense_grad, router_weight, preferred_element_type=F32).astype(BF16)
    router_part = lax.dot_general(
        dense_grad, inputs, (((0,), (0,)), ((), ())), preferred_element_type=F32
    )
    router_grad = lax.psum(router_part, ("dp", "expert"))
    return (hidden_grad, down_grad, input_grad, router_grad)


INNER = [(1, 2), (2, 1)]
FAR = [(0, 2), (3, 1)]
OUTER = [(0, 1), (3, 2)]
OUTWARD = [(1, 0), (2, 3)]


def plane_swap(x, bits):
    return lax.ppermute(x, "expert", [(i, i ^ bits) for i in range(8)])


def plane_blocks(x, across, along, stacked, diagonal):
    swapped = plane_swap(stacked, 1)
    corner = [plane_swap(piece, 1) for piece in diagonal]
    return [
        [(x, None)],
        [(swapped, 0)],
        [(across, None)],
        [(swapped, 1)],
        [(along, None)],
        [(swapped, 2)],
        [(piece, None) for piece in diagonal],
        [(piece, None) for piece in corner],
    ]


def plane_diagonal(halves):
    return plane_swap(halves[0], 4), plane_swap(halves[1], 2)


def dense_routes(routes, combine, total_experts):
    marks = make_marks(routes, total_experts)
    counts = jnp.sum(marks.astype(F32), axis=1)
    token_order = jnp.arange(routes.shape[0], dtype=jnp.int32)
    earlier = (token_order[None, :] < token_order[:, None]).astype(BF16)
    before = jnp.dot(earlier, counts.astype(BF16), preferred_element_type=F32)
    routed = counts > 0.0
    weights = jnp.sum(jnp.where(marks, combine[:, :, None], 0.0), axis=1)
    return routed, jnp.where(routed, before, -1.0), weights


def describe(positions, weights):
    high = lax.reduce_precision(weights, 8, 7)
    middle = lax.reduce_precision(weights - high, 8, 7)
    low = weights - high - middle
    stacked = jnp.concatenate([positions, high, middle, low], axis=1)
    return stacked.T.astype(BF16)


def pick_rows(owner, local_experts, total_experts):
    row = lax.broadcasted_iota(jnp.int32, (KINDS * local_experts, LANES), 0)
    column = lax.broadcasted_iota(jnp.int32, (KINDS * local_experts, LANES), 1)
    wanted = (row // local_experts) * total_experts + owner * local_experts + row % local_experts
    return (column == wanted).astype(BF16)


def place_rows(ref, start, width, picker, local_experts, capacity, step, store):
    notes = jnp.dot(
        picker, read_block(ref, start + width, start + width + LANES), preferred_element_type=F32
    )
    slots = lax.broadcasted_iota(jnp.int32, (capacity, LANES), 0).astype(F32)
    marks = []
    scales = []
    for expert in range(local_experts):
        weight = (
            notes[local_experts + expert : local_experts + expert + 1]
            + notes[2 * local_experts + expert : 2 * local_experts + expert + 1]
            + notes[3 * local_experts + expert : 3 * local_experts + expert + 1]
        )
        hit = slots == notes[expert : expert + 1]
        marks.append(jnp.where(hit, 1.0, 0.0).astype(BF16))
        scales.append(jnp.sum(jnp.where(hit, weight, 0.0), axis=1, keepdims=True))
    mark = jnp.concatenate(marks, axis=0)
    scale = jnp.concatenate(scales, axis=0)
    for column in range(0, width, step):
        rows = jnp.dot(
            mark,
            read_block(ref, start + column, start + column + step),
            preferred_element_type=F32,
        )
        rows = (rows * scale).astype(BF16)
        for expert in range(local_experts):
            store(expert, column, step, rows[expert * capacity : (expert + 1) * capacity])


def read_block(block, start, stop):
    pieces = []
    for ref, index in block:
        pieces.append(ref[:, start:stop] if index is None else ref[index, :, start:stop])
    return jnp.concatenate(pieces, axis=0) if len(pieces) > 1 else pieces[0]


def arrays_of(blocks):
    arrays = []
    layout = []
    for block in blocks:
        pieces = []
        for array, index in block:
            found = [i for i, known in enumerate(arrays) if known is array]
            if not found:
                arrays.append(array)
                found = [len(arrays) - 1]
            pieces.append((found[0], index))
        layout.append(pieces)
    return arrays, layout


def blocks_of(refs, layout):
    return [[(refs[place], index) for place, index in pieces] for pieces in layout]


def hidden_kernel(
    local_experts, total_experts, capacity, width, part, n_blocks, layout, n_after, place, *refs
):
    blocks = blocks_of(refs[:n_blocks], layout)
    weight_ref, acts_ref = refs[n_blocks : n_blocks + 2]
    hidden_ref, products_ref, near_ref = refs[n_blocks + 2 + n_after :][:3]
    rows = refs[-1]
    expert = pl.program_id(0)
    me = place[0]

    @pl.when(expert == 0)
    def _():
        picker = pick_rows(me, local_experts, total_experts)
        for k in range(8):
            base = pl.multiple_of((me ^ k) * capacity, 16)

            def store(e, column, step, value, base=base):
                rows[e, pl.ds(base, capacity), column : column + step] = value

            place_rows(blocks[k], 0, width, picker, local_experts, capacity, 512, store)

    hidden = jnp.dot(rows[expert], weight_ref[0], preferred_element_type=F32)
    hidden_ref[0] = hidden.astype(BF16)
    product = hidden * acts_ref[0].astype(F32)
    sums = jnp.sum(product.reshape(8, capacity, product.shape[1]), axis=2)
    empty = jnp.zeros((8, LANES - capacity), F32)
    products_ref[0] = jnp.concatenate([sums, empty], axis=1)
    own = pl.multiple_of(place[1] * part, LANES)
    other = pl.multiple_of(place[2] * part, LANES)
    near_ref[0, :, :part] = rows[expert, :, pl.ds(own, part)]
    near_ref[0, :, part:] = rows[expert, :, pl.ds(other, part)]


def whole_block(shape):
    return pl.BlockSpec(shape, lambda *_: (0,) * len(shape))


def hidden_call(place, blocks, weight, acts, total_experts, capacity, part, after, through):
    local_experts, width, hidden_width = weight.shape
    slots = acts.shape[1]
    flat, layout = arrays_of(blocks)
    kernel = functools.partial(
        hidden_kernel,
        local_experts,
        total_experts,
        capacity,
        width,
        part,
        len(flat),
        layout,
        len(after) + len(through),
    )
    tokens = flat[0]
    n_before = 1 + len(flat) + 2 + len(after)
    return pl.pallas_call(
        kernel,
        grid_spec=pltpu.PrefetchScalarGridSpec(
            num_scalar_prefetch=1,
            grid=(local_experts,),
            in_specs=[whole_block(b.shape) for b in flat]
            + [
                pl.BlockSpec((1, width, hidden_width), lambda e, p: (e, 0, 0)),
                pl.BlockSpec((1, slots, hidden_width), lambda e, p: (e, 0, 0)),
            ]
            + [ANYWHERE] * (len(after) + len(through)),
            out_specs=[
                pl.BlockSpec((1, slots, hidden_width), lambda e, p: (e, 0, 0)),
                pl.BlockSpec((1, 8, LANES), lambda e, p: (e, 0, 0)),
                pl.BlockSpec((1, slots, 2 * part), lambda e, p: (e, 0, 0)),
            ]
            + [ANYWHERE] * len(through),
            scratch_shapes=[pltpu.VMEM((local_experts, slots, width), BF16)],
        ),
        out_shape=[
            jax.ShapeDtypeStruct((local_experts, slots, hidden_width), BF16),
            jax.ShapeDtypeStruct((local_experts, 8, LANES), F32),
            jax.ShapeDtypeStruct((local_experts, slots, 2 * part), BF16),
        ]
        + [jax.ShapeDtypeStruct(array.shape, array.dtype) for array in through],
        input_output_aliases={n_before + i: 3 + i for i in range(len(through))},
        compiler_params=pltpu.CompilerParams(vmem_limit_bytes=56 * MIB),
        cost_estimate=pl.CostEstimate(
            flops=2 * local_experts * slots * width * (hidden_width + 256),
            bytes_accessed=2 * (weight.size + 2 * acts.size + 10 * tokens.size),
            transcendentals=0,
        ),
        name="hidden_and_products",
    )(place, *flat, weight, acts, *after, *through)


def rows_kernel(
    local_experts, total_experts, capacity, widths, n_blocks, layout, n_after, place, *refs
):
    blocks = blocks_of(refs[:n_blocks], layout)
    outs = refs[n_blocks + n_after : n_blocks + n_after + local_experts]
    rows, stored = refs[n_blocks + n_after + local_experts :]
    slots = 8 * capacity
    me = place[0]
    picker = pick_rows(me, local_experts, total_experts)
    start = 0
    stores = []
    for index, width in enumerate(widths):
        for k in range(8):
            base = pl.multiple_of(index * slots + (me ^ k) * capacity, 16)

            def store(e, column, step, value, base=base):
                rows[e, pl.ds(base, capacity), column : column + step] = value

            place_rows(blocks[k], start, width, picker, local_experts, capacity, 512, store)
        start += width + LANES
        group = pl.ds(index * slots, slots)
        for expert in range(local_experts):
            held = rows.at[expert, group]
            target = outs[expert].at[group]
            stores.append(pltpu.make_async_copy(held, target, stored.at[index, expert]))
            stores[-1].start()
    for copy in stores:
        copy.wait()


def rows_call(place, blocks, widths, local_experts, total_experts, capacity, after):
    flat, layout = arrays_of(blocks)
    shape = (len(widths) * 8 * capacity, widths[0])
    kernel = functools.partial(
        rows_kernel,
        local_experts,
        total_experts,
        capacity,
        widths,
        len(flat),
        layout,
        len(after),
    )
    return pl.pallas_call(
        kernel,
        in_specs=[pl.BlockSpec(memory_space=pltpu.SMEM)]
        + [pl.BlockSpec(memory_space=pltpu.VMEM)] * len(flat)
        + [ANYWHERE] * len(after),
        out_specs=[pl.BlockSpec(memory_space=pltpu.VMEM)] + [ANYWHERE] * (local_experts - 1),
        out_shape=[pltpu.VMEM(shape, BF16)]
        + [jax.ShapeDtypeStruct(shape, BF16)] * (local_experts - 1),
        scratch_shapes=[
            pltpu.VMEM((local_experts, *shape), BF16),
            pltpu.SemaphoreType.DMA((len(widths), local_experts)),
        ],
        compiler_params=pltpu.CompilerParams(vmem_limit_bytes=56 * MIB),
        cost_estimate=pl.CostEstimate(
            flops=2 * local_experts * 8 * capacity * 256 * sum(widths),
            bytes_accessed=2 * local_experts * shape[0] * shape[1],
            transcendentals=0,
        ),
        name="far_rows",
    )(place, *flat, *after)


def copy_kernel(moves, first_target, *refs):
    targets = refs[first_target : first_target + len(moves)]
    for target, pieces in zip(targets, moves):
        for source, source_index, target_index in pieces:
            target[target_index] = refs[source][source_index]


def copies(name, sources, results, moves, after, vmem_limit):
    vmem = pl.BlockSpec(memory_space=pltpu.VMEM)
    return pl.pallas_call(
        functools.partial(copy_kernel, moves, len(sources) + len(after)),
        in_specs=[vmem] * len(sources) + [ANYWHERE] * len(after),
        out_specs=[vmem] * len(results),
        out_shape=[jax.ShapeDtypeStruct(shape, BF16) for shape in results],
        compiler_params=pltpu.CompilerParams(vmem_limit_bytes=vmem_limit),
        cost_estimate=pl.CostEstimate(
            flops=0,
            bytes_accessed=4 * sum(array.size for array in sources),
            transcendentals=0,
        ),
        name=name,
    )(*sources, *after)


def nothing_kernel(*_):
    pass


def held_until(arrays, after):
    return pl.pallas_call(
        nothing_kernel,
        in_specs=[ANYWHERE] * (len(arrays) + len(after)),
        out_specs=[ANYWHERE] * len(arrays),
        out_shape=[jax.ShapeDtypeStruct(array.shape, array.dtype) for array in arrays],
        input_output_aliases={i: i for i in range(len(arrays))},
        compiler_params=pltpu.CompilerParams(has_side_effects=True),
        cost_estimate=SMALL,
        name="held_until",
    )(*arrays, *after)


def rows_of(start, stop):
    return (slice(start, stop), slice(None))


def columns_of(start, stop):
    return (slice(None), slice(start, stop))


def outer_product(rows, acts):
    return lax.dot_general(rows, acts, (((0,), (0,)), ((), ())), preferred_element_type=F32)


def down_kernel(places, n_after, rows, *refs):
    sources = refs[:5]
    own_ref, other_ref, near, acts, results, loaded, stored = refs[5 + n_after :]
    slots, width = near.shape
    part = width // 2
    targets = [near] + [acts.at[pl.ds(i * slots, slots)] for i in range(4)]
    loads = [
        pltpu.make_async_copy(source.at[place], target, loaded.at[i])
        for i, (source, place, target) in enumerate(zip(sources, places, targets))
    ]
    for load in loads:
        load.start()
    stores = [
        pltpu.make_async_copy(results.at[i], target, stored.at[i])
        for i, target in enumerate((other_ref, own_ref))
    ]
    for load in loads[:4]:
        load.wait()
    total = outer_product(near[:, part:], acts[:slots])
    total += outer_product(rows[: 2 * slots, part:], acts[slots : 3 * slots])
    results[0] = total.astype(BF16)
    stores[0].start()
    loads[4].wait()
    total = outer_product(near[:, :part], acts[:slots])
    total += outer_product(rows[:, :part], acts[slots:])
    results[1] = total.astype(BF16)
    stores[1].start()
    for store in stores:
        store.wait()


def down_call(rows, near, acts, after):
    sources = [near, *acts]
    arrays = [array for array, _ in sources]
    places = [place for _, place in sources]
    slots, hidden_width = arrays[1].shape[1:]
    width = rows.shape[1]
    return pl.pallas_call(
        functools.partial(down_kernel, places, len(after)),
        in_specs=[pl.BlockSpec(memory_space=pltpu.VMEM)]
        + [ANYWHERE] * (len(arrays) + len(after)),
        out_specs=[ANYWHERE] * 2,
        out_shape=[jax.ShapeDtypeStruct((width // 2, hidden_width), BF16)] * 2,
        scratch_shapes=[
            pltpu.VMEM((slots, width), BF16),
            pltpu.VMEM((4 * slots, hidden_width), BF16),
            pltpu.VMEM((2, width // 2, hidden_width), BF16),
            pltpu.SemaphoreType.DMA((5,)),
            pltpu.SemaphoreType.DMA((2,)),
        ],
        compiler_params=pltpu.CompilerParams(vmem_limit_bytes=50 * MIB),
        cost_estimate=SMALL,
        name="down_terms",
    )(pltpu.with_memory_space_constraint(rows, pltpu.VMEM), *arrays, *after)


def router_kernel(total_experts, n_after, products, places, weights, gate, inputs, *refs):
    input_ref, part_ref = refs[n_after:]
    by_slot = products[...]
    capacity = by_slot.shape[1]
    slots = lax.broadcasted_iota(jnp.int32, (capacity, places.shape[1]), 0).astype(F32)
    sums = []
    for expert in range(total_experts):
        hit = slots == places[expert : expert + 1, :]
        sums.append(
            jnp.sum(jnp.where(hit, by_slot[expert][:, None], 0.0), axis=0, keepdims=True)
        )
    pair_sums = jnp.concatenate(sums, axis=0)
    logits = pair_sums - weights[...] * jnp.sum(pair_sums, axis=0, keepdims=True)
    dense = jnp.where(places[...] >= 0.0, logits, 0.0).astype(BF16)
    step = part_ref.shape[2]
    for index in range(part_ref.shape[0]):
        columns = inputs[:, index * step : (index + 1) * step]
        part_ref[index] = jnp.dot(dense, columns, preferred_element_type=F32)
    input_ref[...] = lax.dot_general(
        dense, gate[...], (((0,), (0,)), ((), ())), preferred_element_type=F32
    ).astype(BF16)


def router_call(products, places, weights, gate, inputs, after):
    vmem = pl.BlockSpec(memory_space=pltpu.VMEM)
    return pl.pallas_call(
        functools.partial(router_kernel, gate.shape[0], len(after)),
        in_specs=[vmem] * 5 + [ANYWHERE] * len(after),
        out_specs=[vmem] * 2,
        out_shape=[
            jax.ShapeDtypeStruct(inputs.shape, BF16),
            jax.ShapeDtypeStruct((8, gate.shape[0], gate.shape[1] // 8), F32),
        ],
        compiler_params=pltpu.CompilerParams(vmem_limit_bytes=24 * MIB),
        cost_estimate=SMALL,
        name="router_terms",
    )(products, places, weights, gate, inputs, *after)


def sum_kernel(*refs):
    own, first, second, third = refs[:4]
    refs[-1][...] = (own[...] + first[...]) + (second[...] + third[...])


def sum_planes(x, others, after):
    vmem = pl.BlockSpec(memory_space=pltpu.VMEM)
    return pl.pallas_call(
        sum_kernel,
        in_specs=[vmem] * 4 + [ANYWHERE] * len(after),
        out_specs=vmem,
        out_shape=jax.ShapeDtypeStruct(x.shape, x.dtype),
        cost_estimate=SMALL,
        name="sum_planes",
    )(x, *others, *after)


def local_line(inputs, out_grad, combine, routes, saved_hidden, down_weight, router_weight):
    width = out_grad.shape[1]
    local_experts = down_weight.shape[0]
    total_experts = router_weight.shape[0]
    capacity = saved_hidden.shape[3]
    hidden_width = saved_hidden.shape[4]
    slots = 8 * capacity
    part = width // 4
    plane = lax.axis_index("dp")
    member = lax.axis_index("expert")
    lower = plane < 2
    acts = saved_hidden.reshape(local_experts, slots, hidden_width)

    routed, positions, weights = dense_routes(routes, combine, total_experts)
    notes = describe(positions, weights)
    parts = [out_grad[:, i * part : (i + 1) * part] for i in range(4)]

    pair = jnp.concatenate(
        [jnp.where(lower, parts[2], parts[1]), jnp.where(lower, parts[3], parts[0]), notes], axis=1
    )
    single = jnp.concatenate([jnp.where(lower, parts[1], parts[2]), notes], axis=1)
    from_inner = lax.ppermute(pair, "dp", INNER)
    from_far = lax.ppermute(pair, "dp", FAR)
    from_outer = lax.ppermute(single, "dp", OUTER)

    other_part = jnp.where(lower, 0, 3)
    place = jnp.stack([member, plane, other_part]).astype(jnp.int32)

    tokens = jnp.concatenate([out_grad, notes], axis=1)
    across = plane_swap(tokens, 2)
    along = plane_swap(tokens, 4)
    n_tokens = tokens.shape[0]
    half = n_tokens // 2

    groups = [(0, 2), (2, local_experts)]
    acts_early, *acts_late = copies(
        "acts_pieces",
        [acts],
        [(stop - start, slots, hidden_width) for start, stop in groups],
        [[(0, slice(start, stop), Ellipsis)] for start, stop in groups],
        [across],
        60 * MIB,
    )
    *halves, stacked = copies(
        "first_pieces",
        [across, along, tokens],
        [(half, tokens.shape[1])] * 2 + [(3, *tokens.shape)],
        [[(0, rows_of(0, half), Ellipsis)], [(1, rows_of(half, n_tokens), Ellipsis)]]
        + [[(source, Ellipsis, index) for index, source in enumerate((2, 0, 1))]],
        [from_inner, from_far, from_outer, acts_early],
        60 * MIB,
    )
    diagonal = plane_diagonal(halves)
    own_blocks = plane_blocks(tokens, across, along, stacked, diagonal)
    inners = [lax.ppermute(acts_early, "dp", INNER)]
    outers = [lax.ppermute(acts_early, "dp", OUTER)]

    widths = [block.shape[1] for block in (from_inner, from_far, from_outer)]
    starts = [sum(widths[:i]) for i in range(3)]
    (columns,) = copies(
        "side_by_side",
        [from_inner, from_far, from_outer],
        [(n_tokens, sum(widths))],
        [[(i, Ellipsis, columns_of(starts[i], starts[i] + widths[i])) for i in range(3)]],
        diagonal,
        60 * MIB,
    )
    columns_across = plane_swap(columns, 2)
    columns_along = plane_swap(columns, 4)

    hidden, products, near, *late = hidden_call(
        place, own_blocks, down_weight, acts, total_experts, capacity, part,
        [columns], acts_late,
    )
    inners += [lax.ppermute(a, "dp", INNER) for a in late]
    outers += [lax.ppermute(a, "dp", OUTER) for a in late]
    fars = [lax.ppermute(outers[0], "dp", INNER)]
    fars += [
        lax.ppermute(outers[1][i : i + 1], "dp", INNER) for i in range(local_experts - 2)
    ]

    *column_halves, stacked = copies(
        "second_pieces",
        [columns_across, columns_along, columns],
        [(half, sum(widths))] * 2 + [(3, *columns.shape)],
        [[(0, rows_of(0, half), Ellipsis)], [(1, rows_of(half, n_tokens), Ellipsis)]]
        + [[(source, Ellipsis, index) for index, source in enumerate((2, 0, 1))]],
        [hidden, outers[0], inners[0]],
        56 * MIB,
    )
    (products,) = held_until([products], column_halves)
    returned = lax.all_to_all(
        products.transpose(1, 0, 2), "expert", split_axis=0, concat_axis=0
    ).reshape(total_experts, LANES)
    input_grad, router_part = router_call(
        returned, positions.T, weights.T, router_weight, inputs, []
    )
    corner = held_until(plane_diagonal(column_halves), [router_part])
    other_blocks = plane_blocks(columns, columns_across, columns_along, stacked, corner)
    rows = rows_call(
        place, other_blocks, (2 * part, 2 * part, part), local_experts, total_experts, capacity, []
    )

    def down(expert, after, hold=()):
        group, place = divmod(expert, 2)
        far = (fars[0], expert) if expert < 2 else (fars[expert - 1], 0)
        pieces = [(acts, expert), (inners[group], place), far, (outers[group], place)]
        own, other = down_call(rows[expert], (near, expert), pieces, after)
        if hold:
            (other,) = held_until([other], hold)
        return own, lax.ppermute(other, "dp", OUTWARD)

    def finish(own, came):
        return (own.astype(F32) + came.astype(F32)).astype(BF16)

    downs = [down(0, [])]
    downs.append(down(1, [downs[0][0]]))
    reduced = jnp.sum(
        lax.all_to_all(router_part, "expert", split_axis=0, concat_axis=0), axis=0
    )
    downs.append(down(2, [downs[1][0], inners[1], downs[0][1]]))
    others = [lax.ppermute(reduced, "dp", [(i, i ^ k) for i in range(4)]) for k in (1, 2, 3)]
    finished = [finish(*downs[0])]
    downs.append(down(3, [downs[2][0], *finished, *others]))
    finished += [finish(*downs[expert]) for expert in range(1, 4)]
    summed = sum_planes(reduced, others, [downs[-1][0]])
    router_grad = (
        lax.all_gather(summed, "expert").transpose(1, 0, 2).reshape(total_experts, width)
    )

    down_grad = jnp.stack(finished)

    hidden_grad = hidden.reshape(saved_hidden.shape)
    return (hidden_grad, down_grad, input_grad, router_grad)


def solution(mesh):
    in_line = mesh.shape["dp"] == 4 and mesh.shape["expert"] == 8

    def local(inputs, out_grad, combine, routes, saved_hidden, down_weight, router_weight):
        tokens, width = out_grad.shape
        fits = (
            in_line
            and tokens == LANES
            and KINDS * router_weight.shape[0] == LANES
            and width % 2048 == 0
            and saved_hidden.shape[3] % 16 == 0
            and saved_hidden.shape[4] % LANES == 0
        )
        body = local_line if fits else local_any
        return body(
            inputs, out_grad, combine, routes, saved_hidden, down_weight, router_weight
        )

    placed = (
        P(("dp", "expert"), None),
        P(("dp", "expert"), None),
        P(("dp", "expert"), None),
        P(("dp", "expert"), None),
        P("dp", "expert", None, None, None),
        P("expert", None, None),
        P(),
    )
    return jax.shard_map(
        local,
        mesh=mesh,
        in_specs=placed,
        out_specs=(
            P("dp", "expert", None, None, None),
            P("expert", "dp", None),
            P(("dp", "expert"), None),
            P(),
        ),
        check_vma=False,
    )
```

```python
import functools

import jax
import jax.numpy as jnp
from jax import lax
from jax.experimental import pallas as pl
from jax.experimental.pallas import tpu as pltpu
from jax.sharding import PartitionSpec as P

F32 = jnp.float32
BF16 = jnp.bfloat16
LANES = 128
KINDS = 4
MIB = 1024 * 1024
VMEM_LIMIT = 51 * MIB
ANYWHERE = pl.BlockSpec(memory_space=pl.ANY)
SMALL = pl.CostEstimate(flops=1000, bytes_accessed=1000, transcendentals=0)


def make_marks(block_routes, total_experts):
    return block_routes[:, :, None] == jnp.arange(total_experts, dtype=jnp.int32)[None, None, :]


def slot_positions(route_marks):
    counts = jnp.sum(route_marks.astype(BF16), axis=1)
    token_order = jnp.arange(route_marks.shape[0], dtype=jnp.int32)
    earlier = (token_order[None, :] < token_order[:, None]).astype(BF16)
    before = jnp.dot(earlier, counts, preferred_element_type=F32)
    picked = jnp.sum(jnp.where(route_marks, before[:, None, :], 0.0), axis=2)
    return picked.astype(jnp.int32)


def pack_rows(scaled, lane_index, owner_slot, positions, local_experts, groups, capacity):
    width = scaled.shape[-1]
    flat_index = (owner_slot * groups + lane_index) * capacity + positions
    zero_rows = jnp.zeros((local_experts * groups * capacity, width), BF16)
    filled = zero_rows.at[flat_index.reshape(-1)].set(scaled.reshape(-1, width))
    return filled.reshape(local_experts, groups, capacity, width)


def local_any(inputs, out_grad, combine, routes, saved_hidden, down_weight, router_weight):
    token_count, width = out_grad.shape
    local_experts = down_weight.shape[0]
    total_experts = router_weight.shape[0]
    groups = lax.axis_size("expert")
    capacity = saved_hidden.shape[3]
    hidden_width = saved_hidden.shape[4]
    route_marks = make_marks(routes, total_experts)
    positions = slot_positions(route_marks)
    owner_dev = routes // local_experts
    owner_slot = routes % local_experts
    scaled = (combine[:, :, None] * out_grad[:, None, :].astype(F32)).astype(BF16)
    packed = pack_rows(scaled, owner_dev, owner_slot, positions, local_experts, groups, capacity)
    received = lax.all_to_all(packed, "expert", split_axis=1, concat_axis=1, tiled=True)
    hidden_local = saved_hidden[0]
    products_list = []
    hidden_list = []
    weight_terms = []
    for expert in range(local_experts):
        slot_rows = received[expert].reshape(groups * capacity, width)
        slot_acts = hidden_local[expert].reshape(groups * capacity, hidden_width)
        weight = down_weight[expert]
        hidden = jnp.dot(slot_rows, weight, preferred_element_type=F32)
        products_list.append(jnp.sum(hidden * slot_acts.astype(F32), axis=1))
        hidden_list.append(hidden.astype(BF16))
        weight_terms.append(
            lax.dot_general(
                slot_rows, slot_acts, (((0,), (0,)), ((), ())), preferred_element_type=F32
            )
        )
    down_grad = lax.psum_scatter(
        jnp.stack(weight_terms).astype(BF16), "dp", scatter_dimension=1, tiled=True
    )
    hidden_grad = jnp.stack(hidden_list).reshape(1, local_experts, groups, capacity, hidden_width)
    slot_products = jnp.stack(products_list).reshape(local_experts, groups, capacity)
    returned = lax.all_to_all(slot_products, "expert", split_axis=1, concat_axis=1, tiled=True)
    pair_index = (owner_slot * groups + owner_dev) * capacity + positions
    pair_sums = returned.reshape(-1)[pair_index]
    logit_grad = pair_sums - combine * jnp.sum(pair_sums, axis=1, keepdims=True)
    dense_grad = jnp.sum(jnp.where(route_marks, logit_grad[:, :, None], 0.0), axis=1).astype(BF16)
    input_grad = jnp.dot(dense_grad, router_weight, preferred_element_type=F32).astype(BF16)
    router_part = lax.dot_general(
        dense_grad, inputs, (((0,), (0,)), ((), ())), preferred_element_type=F32
    )
    router_grad = lax.psum(router_part, ("dp", "expert"))
    return (hidden_grad, down_grad, input_grad, router_grad)


INNER = [(1, 2), (2, 1)]
FAR = [(0, 2), (3, 1)]
OUTER = [(0, 1), (3, 2)]
OUTWARD = [(1, 0), (2, 3)]


def plane_swap(x, bits):
    return lax.ppermute(x, "expert", [(i, i ^ bits) for i in range(8)])


def plane_blocks(x, across, along, stacked, diagonal):
    swapped = plane_swap(stacked, 1)
    corner = [plane_swap(piece, 1) for piece in diagonal]
    return [
        [(x, None)],
        [(swapped, 0)],
        [(across, None)],
        [(swapped, 1)],
        [(along, None)],
        [(swapped, 2)],
        [(piece, None) for piece in diagonal],
        [(piece, None) for piece in corner],
    ]


def plane_diagonal(halves):
    return plane_swap(halves[0], 4), plane_swap(halves[1], 2)


def dense_routes(routes, combine, total_experts):
    marks = make_marks(routes, total_experts)
    counts = jnp.sum(marks.astype(F32), axis=1)
    token_order = jnp.arange(routes.shape[0], dtype=jnp.int32)
    earlier = (token_order[None, :] < token_order[:, None]).astype(BF16)
    before = jnp.dot(earlier, counts.astype(BF16), preferred_element_type=F32)
    routed = counts > 0.0
    weights = jnp.sum(jnp.where(marks, combine[:, :, None], 0.0), axis=1)
    return routed, jnp.where(routed, before, -1.0), weights


def describe(positions, weights):
    high = lax.reduce_precision(weights, 8, 7)
    middle = lax.reduce_precision(weights - high, 8, 7)
    low = weights - high - middle
    stacked = jnp.concatenate([positions, high, middle, low], axis=1)
    return stacked.T.astype(BF16)


def pick_rows(owner, local_experts, total_experts):
    row = lax.broadcasted_iota(jnp.int32, (KINDS * local_experts, LANES), 0)
    column = lax.broadcasted_iota(jnp.int32, (KINDS * local_experts, LANES), 1)
    wanted = (row // local_experts) * total_experts + owner * local_experts + row % local_experts
    return (column == wanted).astype(BF16)


def place_rows(ref, start, width, picker, local_experts, capacity, step, store):
    notes = jnp.dot(
        picker, read_block(ref, start + width, start + width + LANES), preferred_element_type=F32
    )
    slots = lax.broadcasted_iota(jnp.int32, (capacity, LANES), 0).astype(F32)
    marks = []
    scales = []
    for expert in range(local_experts):
        weight = (
            notes[local_experts + expert : local_experts + expert + 1]
            + notes[2 * local_experts + expert : 2 * local_experts + expert + 1]
            + notes[3 * local_experts + expert : 3 * local_experts + expert + 1]
        )
        hit = slots == notes[expert : expert + 1]
        marks.append(jnp.where(hit, 1.0, 0.0).astype(BF16))
        scales.append(jnp.sum(jnp.where(hit, weight, 0.0), axis=1, keepdims=True))
    mark = jnp.concatenate(marks, axis=0)
    scale = jnp.concatenate(scales, axis=0)
    for column in range(0, width, step):
        rows = jnp.dot(
            mark,
            read_block(ref, start + column, start + column + step),
            preferred_element_type=F32,
        )
        rows = (rows * scale).astype(BF16)
        for expert in range(local_experts):
            store(expert, column, step, rows[expert * capacity : (expert + 1) * capacity])


def read_block(block, start, stop):
    pieces = []
    for ref, index in block:
        pieces.append(ref[:, start:stop] if index is None else ref[index, :, start:stop])
    return jnp.concatenate(pieces, axis=0) if len(pieces) > 1 else pieces[0]


def arrays_of(blocks):
    arrays = []
    layout = []
    for block in blocks:
        pieces = []
        for array, index in block:
            found = [i for i, known in enumerate(arrays) if known is array]
            if not found:
                arrays.append(array)
                found = [len(arrays) - 1]
            pieces.append((found[0], index))
        layout.append(pieces)
    return arrays, layout


def blocks_of(refs, layout):
    return [[(refs[place], index) for place, index in pieces] for pieces in layout]


def hidden_kernel(
    local_experts, total_experts, capacity, width, part, n_blocks, layout, n_after, place, *refs
):
    blocks = blocks_of(refs[:n_blocks], layout)
    weight_ref, acts_ref = refs[n_blocks : n_blocks + 2]
    hidden_ref, products_ref, near_ref = refs[n_blocks + 2 + n_after :][:3]
    rows = refs[-1]
    expert = pl.program_id(0)
    me = place[0]

    @pl.when(expert == 0)
    def _():
        picker = pick_rows(me, local_experts, total_experts)
        for k in range(8):
            base = pl.multiple_of((me ^ k) * capacity, 16)

            def store(e, column, step, value, base=base):
                rows[e, pl.ds(base, capacity), column : column + step] = value

            place_rows(blocks[k], 0, width, picker, local_experts, capacity, 512, store)

    hidden = jnp.dot(rows[expert], weight_ref[0], preferred_element_type=F32)
    hidden_ref[0] = hidden.astype(BF16)
    product = hidden * acts_ref[0].astype(F32)
    sums = jnp.sum(product.reshape(8, capacity, product.shape[1]), axis=2)
    empty = jnp.zeros((8, LANES - capacity), F32)
    products_ref[0] = jnp.concatenate([sums, empty], axis=1)
    own = pl.multiple_of(place[1] * part, LANES)
    other = pl.multiple_of(place[2] * part, LANES)
    near_ref[0, :, :part] = rows[expert, :, pl.ds(own, part)]
    near_ref[0, :, part:] = rows[expert, :, pl.ds(other, part)]


def whole_block(shape):
    return pl.BlockSpec(shape, lambda *_: (0,) * len(shape))


def hidden_call(place, blocks, weight, acts, total_experts, capacity, part, after, through):
    local_experts, width, hidden_width = weight.shape
    slots = acts.shape[1]
    flat, layout = arrays_of(blocks)
    kernel = functools.partial(
        hidden_kernel,
        local_experts,
        total_experts,
        capacity,
        width,
        part,
        len(flat),
        layout,
        len(after) + len(through),
    )
    tokens = flat[0]
    n_before = 1 + len(flat) + 2 + len(after)
    return pl.pallas_call(
        kernel,
        grid_spec=pltpu.PrefetchScalarGridSpec(
            num_scalar_prefetch=1,
            grid=(local_experts,),
            in_specs=[whole_block(b.shape) for b in flat]
            + [
                pl.BlockSpec((1, width, hidden_width), lambda e, p: (e, 0, 0)),
                pl.BlockSpec((1, slots, hidden_width), lambda e, p: (e, 0, 0)),
            ]
            + [ANYWHERE] * (len(after) + len(through)),
            out_specs=[
                pl.BlockSpec((1, slots, hidden_width), lambda e, p: (e, 0, 0)),
                pl.BlockSpec((1, 8, LANES), lambda e, p: (e, 0, 0)),
                pl.BlockSpec((1, slots, 2 * part), lambda e, p: (e, 0, 0)),
            ]
            + [ANYWHERE] * len(through),
            scratch_shapes=[pltpu.VMEM((local_experts, slots, width), BF16)],
        ),
        out_shape=[
            jax.ShapeDtypeStruct((local_experts, slots, hidden_width), BF16),
            jax.ShapeDtypeStruct((local_experts, 8, LANES), F32),
            jax.ShapeDtypeStruct((local_experts, slots, 2 * part), BF16),
        ]
        + [jax.ShapeDtypeStruct(array.shape, array.dtype) for array in through],
        input_output_aliases={n_before + i: 3 + i for i in range(len(through))},
        compiler_params=pltpu.CompilerParams(vmem_limit_bytes=56 * MIB),
        cost_estimate=pl.CostEstimate(
            flops=2 * local_experts * slots * width * (hidden_width + 256),
            bytes_accessed=2 * (weight.size + 2 * acts.size + 10 * tokens.size),
            transcendentals=0,
        ),
        name="hidden_and_products",
    )(place, *flat, weight, acts, *after, *through)


def rows_kernel(
    local_experts, total_experts, capacity, widths, n_blocks, layout, n_after, place, *refs
):
    blocks = blocks_of(refs[:n_blocks], layout)
    outs = refs[n_blocks + n_after : n_blocks + n_after + local_experts]
    rows, stored = refs[n_blocks + n_after + local_experts :]
    slots = 8 * capacity
    me = place[0]
    picker = pick_rows(me, local_experts, total_experts)
    start = 0
    stores = []
    for index, width in enumerate(widths):
        for k in range(8):
            base = pl.multiple_of(index * slots + (me ^ k) * capacity, 16)

            def store(e, column, step, value, base=base):
                rows[e, pl.ds(base, capacity), column : column + step] = value

            place_rows(blocks[k], start, width, picker, local_experts, capacity, 512, store)
        start += width + LANES
        group = pl.ds(index * slots, slots)
        for expert in range(local_experts):
            held = rows.at[expert, group]
            target = outs[expert].at[group]
            stores.append(pltpu.make_async_copy(held, target, stored.at[index, expert]))
            stores[-1].start()
    for copy in stores:
        copy.wait()


def rows_call(place, blocks, widths, local_experts, total_experts, capacity, after):
    flat, layout = arrays_of(blocks)
    shape = (len(widths) * 8 * capacity, widths[0])
    kernel = functools.partial(
        rows_kernel,
        local_experts,
        total_experts,
        capacity,
        widths,
        len(flat),
        layout,
        len(after),
    )
    return pl.pallas_call(
        kernel,
        in_specs=[pl.BlockSpec(memory_space=pltpu.SMEM)]
        + [pl.BlockSpec(memory_space=pltpu.VMEM)] * len(flat)
        + [ANYWHERE] * len(after),
        out_specs=[pl.BlockSpec(memory_space=pltpu.VMEM)] * 2 + [ANYWHERE] * (local_experts - 2),
        out_shape=[pltpu.VMEM(shape, BF16)] * 2
        + [jax.ShapeDtypeStruct(shape, BF16)] * (local_experts - 2),
        scratch_shapes=[
            pltpu.VMEM((local_experts, *shape), BF16),
            pltpu.SemaphoreType.DMA((len(widths), local_experts)),
        ],
        compiler_params=pltpu.CompilerParams(vmem_limit_bytes=56 * MIB),
        cost_estimate=pl.CostEstimate(
            flops=2 * local_experts * 8 * capacity * 256 * sum(widths),
            bytes_accessed=2 * local_experts * shape[0] * shape[1],
            transcendentals=0,
        ),
        name="far_rows",
    )(place, *flat, *after)


def copy_kernel(moves, first_target, *refs):
    targets = refs[first_target : first_target + len(moves)]
    for target, pieces in zip(targets, moves):
        for source, source_index, target_index in pieces:
            target[target_index] = refs[source][source_index]


def copies(name, sources, results, moves, after, vmem_limit):
    vmem = pl.BlockSpec(memory_space=pltpu.VMEM)
    return pl.pallas_call(
        functools.partial(copy_kernel, moves, len(sources) + len(after)),
        in_specs=[vmem] * len(sources) + [ANYWHERE] * len(after),
        out_specs=[vmem] * len(results),
        out_shape=[jax.ShapeDtypeStruct(shape, BF16) for shape in results],
        compiler_params=pltpu.CompilerParams(vmem_limit_bytes=vmem_limit),
        cost_estimate=pl.CostEstimate(
            flops=0,
            bytes_accessed=4 * sum(array.size for array in sources),
            transcendentals=0,
        ),
        name=name,
    )(*sources, *after)


def nothing_kernel(*_):
    pass


def held_until(arrays, after):
    return pl.pallas_call(
        nothing_kernel,
        in_specs=[ANYWHERE] * (len(arrays) + len(after)),
        out_specs=[ANYWHERE] * len(arrays),
        out_shape=[jax.ShapeDtypeStruct(array.shape, array.dtype) for array in arrays],
        input_output_aliases={i: i for i in range(len(arrays))},
        compiler_params=pltpu.CompilerParams(has_side_effects=True),
        cost_estimate=SMALL,
        name="held_until",
    )(*arrays, *after)


def rows_of(start, stop):
    return (slice(start, stop), slice(None))


def columns_of(start, stop):
    return (slice(None), slice(start, stop))


def outer_product(rows, acts):
    return lax.dot_general(rows, acts, (((0,), (0,)), ((), ())), preferred_element_type=F32)


def down_kernel(places, n_after, rows, *refs):
    sources = refs[:5]
    own_ref, other_ref, near, acts, results, loaded, stored = refs[5 + n_after :]
    slots, width = near.shape
    part = width // 2
    targets = [near] + [acts.at[pl.ds(i * slots, slots)] for i in range(4)]
    loads = [
        pltpu.make_async_copy(source.at[place], target, loaded.at[i])
        for i, (source, place, target) in enumerate(zip(sources, places, targets))
    ]
    for load in loads:
        load.start()
    stores = [
        pltpu.make_async_copy(results.at[i], target, stored.at[i])
        for i, target in enumerate((other_ref, own_ref))
    ]
    for load in loads[:4]:
        load.wait()
    total = outer_product(near[:, part:], acts[:slots])
    total += outer_product(rows[: 2 * slots, part:], acts[slots : 3 * slots])
    results[0] = total.astype(BF16)
    stores[0].start()
    loads[4].wait()
    total = outer_product(near[:, :part], acts[:slots])
    total += outer_product(rows[:, :part], acts[slots:])
    results[1] = total.astype(BF16)
    stores[1].start()
    for store in stores:
        store.wait()


def down_call(rows, near, acts, after):
    sources = [near, *acts]
    arrays = [array for array, _ in sources]
    places = [place for _, place in sources]
    slots, hidden_width = arrays[1].shape[1:]
    width = rows.shape[1]
    return pl.pallas_call(
        functools.partial(down_kernel, places, len(after)),
        in_specs=[pl.BlockSpec(memory_space=pltpu.VMEM)]
        + [ANYWHERE] * (len(arrays) + len(after)),
        out_specs=[ANYWHERE] * 2,
        out_shape=[jax.ShapeDtypeStruct((width // 2, hidden_width), BF16)] * 2,
        scratch_shapes=[
            pltpu.VMEM((slots, width), BF16),
            pltpu.VMEM((4 * slots, hidden_width), BF16),
            pltpu.VMEM((2, width // 2, hidden_width), BF16),
            pltpu.SemaphoreType.DMA((5,)),
            pltpu.SemaphoreType.DMA((2,)),
        ],
        compiler_params=pltpu.CompilerParams(vmem_limit_bytes=50 * MIB),
        cost_estimate=SMALL,
        name="down_terms",
    )(pltpu.with_memory_space_constraint(rows, pltpu.VMEM), *arrays, *after)


def router_kernel(total_experts, n_after, products, places, weights, gate, inputs, *refs):
    input_ref, part_ref = refs[n_after:]
    by_slot = products[...]
    capacity = by_slot.shape[1]
    slots = lax.broadcasted_iota(jnp.int32, (capacity, places.shape[1]), 0).astype(F32)
    sums = []
    for expert in range(total_experts):
        hit = slots == places[expert : expert + 1, :]
        sums.append(
            jnp.sum(jnp.where(hit, by_slot[expert][:, None], 0.0), axis=0, keepdims=True)
        )
    pair_sums = jnp.concatenate(sums, axis=0)
    logits = pair_sums - weights[...] * jnp.sum(pair_sums, axis=0, keepdims=True)
    dense = jnp.where(places[...] >= 0.0, logits, 0.0).astype(BF16)
    step = part_ref.shape[2]
    for index in range(part_ref.shape[0]):
        columns = inputs[:, index * step : (index + 1) * step]
        part_ref[index] = jnp.dot(dense, columns, preferred_element_type=F32)
    input_ref[...] = lax.dot_general(
        dense, gate[...], (((0,), (0,)), ((), ())), preferred_element_type=F32
    ).astype(BF16)


def router_call(products, places, weights, gate, inputs, after):
    vmem = pl.BlockSpec(memory_space=pltpu.VMEM)
    return pl.pallas_call(
        functools.partial(router_kernel, gate.shape[0], len(after)),
        in_specs=[vmem] * 5 + [ANYWHERE] * len(after),
        out_specs=[vmem] * 2,
        out_shape=[
            jax.ShapeDtypeStruct(inputs.shape, BF16),
            jax.ShapeDtypeStruct((8, gate.shape[0], gate.shape[1] // 8), F32),
        ],
        compiler_params=pltpu.CompilerParams(vmem_limit_bytes=24 * MIB),
        cost_estimate=SMALL,
        name="router_terms",
    )(products, places, weights, gate, inputs, *after)


def sum_kernel(*refs):
    own, first, second, third = refs[:4]
    refs[-1][...] = (own[...] + first[...]) + (second[...] + third[...])


def sum_planes(x, others, after):
    vmem = pl.BlockSpec(memory_space=pltpu.VMEM)
    return pl.pallas_call(
        sum_kernel,
        in_specs=[vmem] * 4 + [ANYWHERE] * len(after),
        out_specs=vmem,
        out_shape=jax.ShapeDtypeStruct(x.shape, x.dtype),
        cost_estimate=SMALL,
        name="sum_planes",
    )(x, *others, *after)


def local_line(inputs, out_grad, combine, routes, saved_hidden, down_weight, router_weight):
    width = out_grad.shape[1]
    local_experts = down_weight.shape[0]
    total_experts = router_weight.shape[0]
    capacity = saved_hidden.shape[3]
    hidden_width = saved_hidden.shape[4]
    slots = 8 * capacity
    part = width // 4
    plane = lax.axis_index("dp")
    member = lax.axis_index("expert")
    lower = plane < 2
    acts = saved_hidden.reshape(local_experts, slots, hidden_width)

    routed, positions, weights = dense_routes(routes, combine, total_experts)
    notes = describe(positions, weights)
    parts = [out_grad[:, i * part : (i + 1) * part] for i in range(4)]

    pair = jnp.concatenate(
        [jnp.where(lower, parts[2], parts[1]), jnp.where(lower, parts[3], parts[0]), notes], axis=1
    )
    single = jnp.concatenate([jnp.where(lower, parts[1], parts[2]), notes], axis=1)
    from_inner = lax.ppermute(pair, "dp", INNER)
    from_far = lax.ppermute(pair, "dp", FAR)
    from_outer = lax.ppermute(single, "dp", OUTER)

    other_part = jnp.where(lower, 0, 3)
    place = jnp.stack([member, plane, other_part]).astype(jnp.int32)

    tokens = jnp.concatenate([out_grad, notes], axis=1)
    across = plane_swap(tokens, 2)
    along = plane_swap(tokens, 4)
    n_tokens = tokens.shape[0]
    half = n_tokens // 2

    groups = [(0, 2), (2, local_experts)]
    acts_early, *acts_late = copies(
        "acts_pieces",
        [acts],
        [(stop - start, slots, hidden_width) for start, stop in groups],
        [[(0, slice(start, stop), Ellipsis)] for start, stop in groups],
        [across],
        60 * MIB,
    )
    *halves, stacked = copies(
        "first_pieces",
        [across, along, tokens],
        [(half, tokens.shape[1])] * 2 + [(3, *tokens.shape)],
        [[(0, rows_of(0, half), Ellipsis)], [(1, rows_of(half, n_tokens), Ellipsis)]]
        + [[(source, Ellipsis, index) for index, source in enumerate((2, 0, 1))]],
        [from_inner, from_far, from_outer, acts_early],
        60 * MIB,
    )
    diagonal = plane_diagonal(halves)
    own_blocks = plane_blocks(tokens, across, along, stacked, diagonal)
    inners = [lax.ppermute(acts_early, "dp", INNER)]
    outers = [lax.ppermute(acts_early, "dp", OUTER)]

    widths = [block.shape[1] for block in (from_inner, from_far, from_outer)]
    starts = [sum(widths[:i]) for i in range(3)]
    (columns,) = copies(
        "side_by_side",
        [from_inner, from_far, from_outer],
        [(n_tokens, sum(widths))],
        [[(i, Ellipsis, columns_of(starts[i], starts[i] + widths[i])) for i in range(3)]],
        diagonal,
        60 * MIB,
    )
    columns_across = plane_swap(columns, 2)
    columns_along = plane_swap(columns, 4)

    hidden, products, near, *late = hidden_call(
        place, own_blocks, down_weight, acts, total_experts, capacity, part,
        [columns], acts_late,
    )
    inners += [lax.ppermute(a, "dp", INNER) for a in late]
    outers += [lax.ppermute(a, "dp", OUTER) for a in late]
    fars = [lax.ppermute(outers[0], "dp", INNER)]
    fars += [
        lax.ppermute(outers[1][i : i + 1], "dp", INNER) for i in range(local_experts - 2)
    ]

    *column_halves, stacked = copies(
        "second_pieces",
        [columns_across, columns_along, columns],
        [(half, sum(widths))] * 2 + [(3, *columns.shape)],
        [[(0, rows_of(0, half), Ellipsis)], [(1, rows_of(half, n_tokens), Ellipsis)]]
        + [[(source, Ellipsis, index) for index, source in enumerate((2, 0, 1))]],
        [hidden, outers[0], inners[0]],
        56 * MIB,
    )
    (products,) = held_until([products], column_halves)
    returned = lax.all_to_all(
        products.transpose(1, 0, 2), "expert", split_axis=0, concat_axis=0
    ).reshape(total_experts, LANES)
    input_grad, router_part = router_call(
        returned, positions.T, weights.T, router_weight, inputs, []
    )
    corner = held_until(plane_diagonal(column_halves), [router_part])
    other_blocks = plane_blocks(columns, columns_across, columns_along, stacked, corner)
    rows = rows_call(
        place, other_blocks, (2 * part, 2 * part, part), local_experts, total_experts, capacity, []
    )

    def down(expert, after, hold=()):
        group, place = divmod(expert, 2)
        far = (fars[0], expert) if expert < 2 else (fars[expert - 1], 0)
        pieces = [(acts, expert), (inners[group], place), far, (outers[group], place)]
        own, other = down_call(rows[expert], (near, expert), pieces, after)
        if hold:
            (other,) = held_until([other], hold)
        return own, lax.ppermute(other, "dp", OUTWARD)

    def finish(own, came):
        return (own.astype(F32) + came.astype(F32)).astype(BF16)

    downs = [down(0, [])]
    downs.append(down(1, [downs[0][0]]))
    reduced = jnp.sum(
        lax.all_to_all(router_part, "expert", split_axis=0, concat_axis=0), axis=0
    )
    downs.append(down(2, [downs[1][0], inners[1], downs[0][1]]))
    others = [lax.ppermute(reduced, "dp", [(i, i ^ k) for i in range(4)]) for k in (1, 2, 3)]
    finished = [finish(*downs[0])]
    downs.append(down(3, [downs[2][0], *finished, *others]))
    finished += [finish(*downs[expert]) for expert in range(1, 4)]
    summed = sum_planes(reduced, others, [downs[-1][0]])
    router_grad = (
        lax.all_gather(summed, "expert").transpose(1, 0, 2).reshape(total_experts, width)
    )

    down_grad = jnp.stack(finished)

    hidden_grad = hidden.reshape(saved_hidden.shape)
    return (hidden_grad, down_grad, input_grad, router_grad)


def solution(mesh):
    in_line = mesh.shape["dp"] == 4 and mesh.shape["expert"] == 8

    def local(inputs, out_grad, combine, routes, saved_hidden, down_weight, router_weight):
        tokens, width = out_grad.shape
        fits = (
            in_line
            and tokens == LANES
            and KINDS * router_weight.shape[0] == LANES
            and width % 2048 == 0
            and saved_hidden.shape[3] % 16 == 0
            and saved_hidden.shape[4] % LANES == 0
        )
        body = local_line if fits else local_any
        return body(
            inputs, out_grad, combine, routes, saved_hidden, down_weight, router_weight
        )

    placed = (
        P(("dp", "expert"), None),
        P(("dp", "expert"), None),
        P(("dp", "expert"), None),
        P(("dp", "expert"), None),
        P("dp", "expert", None, None, None),
        P("expert", None, None),
        P(),
    )
    return jax.shard_map(
        local,
        mesh=mesh,
        in_specs=placed,
        out_specs=(
            P("dp", "expert", None, None, None),
            P("expert", "dp", None),
            P(("dp", "expert"), None),
            P(),
        ),
        check_vma=False,
    )
```

```python
import functools

import jax
import jax.numpy as jnp
from jax import lax
from jax.experimental import pallas as pl
from jax.experimental.pallas import tpu as pltpu
from jax.sharding import PartitionSpec as P

F32 = jnp.float32
BF16 = jnp.bfloat16
LANES = 128
KINDS = 4
MIB = 1024 * 1024
VMEM_LIMIT = 51 * MIB
ANYWHERE = pl.BlockSpec(memory_space=pl.ANY)
SMALL = pl.CostEstimate(flops=1000, bytes_accessed=1000, transcendentals=0)


def make_marks(block_routes, total_experts):
    return block_routes[:, :, None] == jnp.arange(total_experts, dtype=jnp.int32)[None, None, :]


def slot_positions(route_marks):
    counts = jnp.sum(route_marks.astype(BF16), axis=1)
    token_order = jnp.arange(route_marks.shape[0], dtype=jnp.int32)
    earlier = (token_order[None, :] < token_order[:, None]).astype(BF16)
    before = jnp.dot(earlier, counts, preferred_element_type=F32)
    picked = jnp.sum(jnp.where(route_marks, before[:, None, :], 0.0), axis=2)
    return picked.astype(jnp.int32)


def pack_rows(scaled, lane_index, owner_slot, positions, local_experts, groups, capacity):
    width = scaled.shape[-1]
    flat_index = (owner_slot * groups + lane_index) * capacity + positions
    zero_rows = jnp.zeros((local_experts * groups * capacity, width), BF16)
    filled = zero_rows.at[flat_index.reshape(-1)].set(scaled.reshape(-1, width))
    return filled.reshape(local_experts, groups, capacity, width)


def local_any(inputs, out_grad, combine, routes, saved_hidden, down_weight, router_weight):
    token_count, width = out_grad.shape
    local_experts = down_weight.shape[0]
    total_experts = router_weight.shape[0]
    groups = lax.axis_size("expert")
    capacity = saved_hidden.shape[3]
    hidden_width = saved_hidden.shape[4]
    route_marks = make_marks(routes, total_experts)
    positions = slot_positions(route_marks)
    owner_dev = routes // local_experts
    owner_slot = routes % local_experts
    scaled = (combine[:, :, None] * out_grad[:, None, :].astype(F32)).astype(BF16)
    packed = pack_rows(scaled, owner_dev, owner_slot, positions, local_experts, groups, capacity)
    received = lax.all_to_all(packed, "expert", split_axis=1, concat_axis=1, tiled=True)
    hidden_local = saved_hidden[0]
    products_list = []
    hidden_list = []
    weight_terms = []
    for expert in range(local_experts):
        slot_rows = received[expert].reshape(groups * capacity, width)
        slot_acts = hidden_local[expert].reshape(groups * capacity, hidden_width)
        weight = down_weight[expert]
        hidden = jnp.dot(slot_rows, weight, preferred_element_type=F32)
        products_list.append(jnp.sum(hidden * slot_acts.astype(F32), axis=1))
        hidden_list.append(hidden.astype(BF16))
        weight_terms.append(
            lax.dot_general(
                slot_rows, slot_acts, (((0,), (0,)), ((), ())), preferred_element_type=F32
            )
        )
    down_grad = lax.psum_scatter(
        jnp.stack(weight_terms).astype(BF16), "dp", scatter_dimension=1, tiled=True
    )
    hidden_grad = jnp.stack(hidden_list).reshape(1, local_experts, groups, capacity, hidden_width)
    slot_products = jnp.stack(products_list).reshape(local_experts, groups, capacity)
    returned = lax.all_to_all(slot_products, "expert", split_axis=1, concat_axis=1, tiled=True)
    pair_index = (owner_slot * groups + owner_dev) * capacity + positions
    pair_sums = returned.reshape(-1)[pair_index]
    logit_grad = pair_sums - combine * jnp.sum(pair_sums, axis=1, keepdims=True)
    dense_grad = jnp.sum(jnp.where(route_marks, logit_grad[:, :, None], 0.0), axis=1).astype(BF16)
    input_grad = jnp.dot(dense_grad, router_weight, preferred_element_type=F32).astype(BF16)
    router_part = lax.dot_general(
        dense_grad, inputs, (((0,), (0,)), ((), ())), preferred_element_type=F32
    )
    router_grad = lax.psum(router_part, ("dp", "expert"))
    return (hidden_grad, down_grad, input_grad, router_grad)


INNER = [(1, 2), (2, 1)]
FAR = [(0, 2), (3, 1)]
OUTER = [(0, 1), (3, 2)]
OUTWARD = [(1, 0), (2, 3)]


def plane_swap(x, bits):
    return lax.ppermute(x, "expert", [(i, i ^ bits) for i in range(8)])


def plane_blocks(x, across, along, stacked, diagonal):
    swapped = plane_swap(stacked, 1)
    corner = [plane_swap(piece, 1) for piece in diagonal]
    return [
        [(x, None)],
        [(swapped, 0)],
        [(across, None)],
        [(swapped, 1)],
        [(along, None)],
        [(swapped, 2)],
        [(piece, None) for piece in diagonal],
        [(piece, None) for piece in corner],
    ]


def plane_diagonal(halves):
    return plane_swap(halves[0], 4), plane_swap(halves[1], 2)


def dense_routes(routes, combine, total_experts):
    marks = make_marks(routes, total_experts)
    counts = jnp.sum(marks.astype(F32), axis=1)
    token_order = jnp.arange(routes.shape[0], dtype=jnp.int32)
    earlier = (token_order[None, :] < token_order[:, None]).astype(BF16)
    before = jnp.dot(earlier, counts.astype(BF16), preferred_element_type=F32)
    routed = counts > 0.0
    weights = jnp.sum(jnp.where(marks, combine[:, :, None], 0.0), axis=1)
    return routed, jnp.where(routed, before, -1.0), weights


def describe(positions, weights):
    high = lax.reduce_precision(weights, 8, 7)
    middle = lax.reduce_precision(weights - high, 8, 7)
    low = weights - high - middle
    stacked = jnp.concatenate([positions, high, middle, low], axis=1)
    return stacked.T.astype(BF16)


def pick_rows(owner, local_experts, total_experts):
    row = lax.broadcasted_iota(jnp.int32, (KINDS * local_experts, LANES), 0)
    column = lax.broadcasted_iota(jnp.int32, (KINDS * local_experts, LANES), 1)
    wanted = (row // local_experts) * total_experts + owner * local_experts + row % local_experts
    return (column == wanted).astype(BF16)


def place_rows(ref, start, width, picker, local_experts, capacity, step, store):
    notes = jnp.dot(
        picker, read_block(ref, start + width, start + width + LANES), preferred_element_type=F32
    )
    slots = lax.broadcasted_iota(jnp.int32, (capacity, LANES), 0).astype(F32)
    marks = []
    scales = []
    for expert in range(local_experts):
        weight = (
            notes[local_experts + expert : local_experts + expert + 1]
            + notes[2 * local_experts + expert : 2 * local_experts + expert + 1]
            + notes[3 * local_experts + expert : 3 * local_experts + expert + 1]
        )
        hit = slots == notes[expert : expert + 1]
        marks.append(jnp.where(hit, 1.0, 0.0).astype(BF16))
        scales.append(jnp.sum(jnp.where(hit, weight, 0.0), axis=1, keepdims=True))
    mark = jnp.concatenate(marks, axis=0)
    scale = jnp.concatenate(scales, axis=0)
    for column in range(0, width, step):
        rows = jnp.dot(
            mark,
            read_block(ref, start + column, start + column + step),
            preferred_element_type=F32,
        )
        rows = (rows * scale).astype(BF16)
        for expert in range(local_experts):
            store(expert, column, step, rows[expert * capacity : (expert + 1) * capacity])


def read_block(block, start, stop):
    pieces = []
    for ref, index in block:
        pieces.append(ref[:, start:stop] if index is None else ref[index, :, start:stop])
    return jnp.concatenate(pieces, axis=0) if len(pieces) > 1 else pieces[0]


def arrays_of(blocks):
    arrays = []
    layout = []
    for block in blocks:
        pieces = []
        for array, index in block:
            found = [i for i, known in enumerate(arrays) if known is array]
            if not found:
                arrays.append(array)
                found = [len(arrays) - 1]
            pieces.append((found[0], index))
        layout.append(pieces)
    return arrays, layout


def blocks_of(refs, layout):
    return [[(refs[place], index) for place, index in pieces] for pieces in layout]


def hidden_kernel(
    local_experts, total_experts, capacity, width, part, n_blocks, layout, n_after, place, *refs
):
    blocks = blocks_of(refs[:n_blocks], layout)
    weight_ref, acts_ref = refs[n_blocks : n_blocks + 2]
    hidden_ref, products_ref, near_ref = refs[n_blocks + 2 + n_after :][:3]
    rows = refs[-1]
    expert = pl.program_id(0)
    me = place[0]

    @pl.when(expert == 0)
    def _():
        picker = pick_rows(me, local_experts, total_experts)
        for k in range(8):
            base = pl.multiple_of((me ^ k) * capacity, 16)

            def store(e, column, step, value, base=base):
                rows[e, pl.ds(base, capacity), column : column + step] = value

            place_rows(blocks[k], 0, width, picker, local_experts, capacity, 512, store)

    hidden = jnp.dot(rows[expert], weight_ref[0], preferred_element_type=F32)
    hidden_ref[0] = hidden.astype(BF16)
    product = hidden * acts_ref[0].astype(F32)
    sums = jnp.sum(product.reshape(8, capacity, product.shape[1]), axis=2)
    empty = jnp.zeros((8, LANES - capacity), F32)
    products_ref[0] = jnp.concatenate([sums, empty], axis=1)
    own = pl.multiple_of(place[1] * part, LANES)
    other = pl.multiple_of(place[2] * part, LANES)
    near_ref[0, :, :part] = rows[expert, :, pl.ds(own, part)]
    near_ref[0, :, part:] = rows[expert, :, pl.ds(other, part)]


def whole_block(shape):
    return pl.BlockSpec(shape, lambda *_: (0,) * len(shape))


def hidden_call(place, blocks, weight, acts, total_experts, capacity, part, after, through):
    local_experts, width, hidden_width = weight.shape
    slots = acts.shape[1]
    flat, layout = arrays_of(blocks)
    kernel = functools.partial(
        hidden_kernel,
        local_experts,
        total_experts,
        capacity,
        width,
        part,
        len(flat),
        layout,
        len(after) + len(through),
    )
    tokens = flat[0]
    n_before = 1 + len(flat) + 2 + len(after)
    return pl.pallas_call(
        kernel,
        grid_spec=pltpu.PrefetchScalarGridSpec(
            num_scalar_prefetch=1,
            grid=(local_experts,),
            in_specs=[whole_block(b.shape) for b in flat]
            + [
                pl.BlockSpec((1, width, hidden_width), lambda e, p: (e, 0, 0)),
                pl.BlockSpec((1, slots, hidden_width), lambda e, p: (e, 0, 0)),
            ]
            + [ANYWHERE] * (len(after) + len(through)),
            out_specs=[
                pl.BlockSpec((1, slots, hidden_width), lambda e, p: (e, 0, 0)),
                pl.BlockSpec((1, 8, LANES), lambda e, p: (e, 0, 0)),
                pl.BlockSpec((1, slots, 2 * part), lambda e, p: (e, 0, 0)),
            ]
            + [ANYWHERE] * len(through),
            scratch_shapes=[pltpu.VMEM((local_experts, slots, width), BF16)],
        ),
        out_shape=[
            jax.ShapeDtypeStruct((local_experts, slots, hidden_width), BF16),
            jax.ShapeDtypeStruct((local_experts, 8, LANES), F32),
            jax.ShapeDtypeStruct((local_experts, slots, 2 * part), BF16),
        ]
        + [jax.ShapeDtypeStruct(array.shape, array.dtype) for array in through],
        input_output_aliases={n_before + i: 3 + i for i in range(len(through))},
        compiler_params=pltpu.CompilerParams(vmem_limit_bytes=56 * MIB),
        cost_estimate=pl.CostEstimate(
            flops=2 * local_experts * slots * width * (hidden_width + 256),
            bytes_accessed=2 * (weight.size + 2 * acts.size + 10 * tokens.size),
            transcendentals=0,
        ),
        name="hidden_and_products",
    )(place, *flat, weight, acts, *after, *through)


def rows_kernel(
    local_experts, total_experts, capacity, widths, n_blocks, layout, n_after, place, *refs
):
    blocks = blocks_of(refs[:n_blocks], layout)
    outs = refs[n_blocks + n_after : n_blocks + n_after + local_experts]
    rows, stored = refs[n_blocks + n_after + local_experts :]
    slots = 8 * capacity
    me = place[0]
    picker = pick_rows(me, local_experts, total_experts)
    start = 0
    stores = []
    for index, width in enumerate(widths):
        for k in range(8):
            base = pl.multiple_of(index * slots + (me ^ k) * capacity, 16)

            def store(e, column, step, value, base=base):
                rows[e, pl.ds(base, capacity), column : column + step] = value

            place_rows(blocks[k], start, width, picker, local_experts, capacity, 512, store)
        start += width + LANES
        group = pl.ds(index * slots, slots)
        for expert in range(local_experts):
            held = rows.at[expert, group]
            target = outs[expert].at[group]
            stores.append(pltpu.make_async_copy(held, target, stored.at[index, expert]))
            stores[-1].start()
    for copy in stores:
        copy.wait()


def rows_call(place, blocks, widths, local_experts, total_experts, capacity, after):
    flat, layout = arrays_of(blocks)
    shape = (len(widths) * 8 * capacity, widths[0])
    kernel = functools.partial(
        rows_kernel,
        local_experts,
        total_experts,
        capacity,
        widths,
        len(flat),
        layout,
        len(after),
    )
    return pl.pallas_call(
        kernel,
        in_specs=[pl.BlockSpec(memory_space=pltpu.SMEM)]
        + [pl.BlockSpec(memory_space=pltpu.VMEM)] * len(flat)
        + [ANYWHERE] * len(after),
        out_specs=[pl.BlockSpec(memory_space=pltpu.VMEM)] * 3 + [ANYWHERE] * (local_experts - 3),
        out_shape=[pltpu.VMEM(shape, BF16)] * 3
        + [jax.ShapeDtypeStruct(shape, BF16)] * (local_experts - 3),
        scratch_shapes=[
            pltpu.VMEM((local_experts, *shape), BF16),
            pltpu.SemaphoreType.DMA((len(widths), local_experts)),
        ],
        compiler_params=pltpu.CompilerParams(vmem_limit_bytes=44 * MIB),
        cost_estimate=pl.CostEstimate(
            flops=2 * local_experts * 8 * capacity * 256 * sum(widths),
            bytes_accessed=2 * local_experts * shape[0] * shape[1],
            transcendentals=0,
        ),
        name="far_rows",
    )(place, *flat, *after)


def copy_kernel(moves, first_target, *refs):
    targets = refs[first_target : first_target + len(moves)]
    for target, pieces in zip(targets, moves):
        for source, source_index, target_index in pieces:
            target[target_index] = refs[source][source_index]


def copies(name, sources, results, moves, after, vmem_limit):
    vmem = pl.BlockSpec(memory_space=pltpu.VMEM)
    return pl.pallas_call(
        functools.partial(copy_kernel, moves, len(sources) + len(after)),
        in_specs=[vmem] * len(sources) + [ANYWHERE] * len(after),
        out_specs=[vmem] * len(results),
        out_shape=[jax.ShapeDtypeStruct(shape, BF16) for shape in results],
        compiler_params=pltpu.CompilerParams(vmem_limit_bytes=vmem_limit),
        cost_estimate=pl.CostEstimate(
            flops=0,
            bytes_accessed=4 * sum(array.size for array in sources),
            transcendentals=0,
        ),
        name=name,
    )(*sources, *after)


def nothing_kernel(*_):
    pass


def held_until(arrays, after):
    return pl.pallas_call(
        nothing_kernel,
        in_specs=[ANYWHERE] * (len(arrays) + len(after)),
        out_specs=[ANYWHERE] * len(arrays),
        out_shape=[jax.ShapeDtypeStruct(array.shape, array.dtype) for array in arrays],
        input_output_aliases={i: i for i in range(len(arrays))},
        compiler_params=pltpu.CompilerParams(has_side_effects=True),
        cost_estimate=SMALL,
        name="held_until",
    )(*arrays, *after)


def rows_of(start, stop):
    return (slice(start, stop), slice(None))


def columns_of(start, stop):
    return (slice(None), slice(start, stop))


def outer_product(rows, acts):
    return lax.dot_general(rows, acts, (((0,), (0,)), ((), ())), preferred_element_type=F32)


def down_kernel(places, n_after, rows, *refs):
    sources = refs[:5]
    own_ref, other_ref, near, acts, results, loaded, stored = refs[5 + n_after :]
    slots, width = near.shape
    part = width // 2
    targets = [near] + [acts.at[pl.ds(i * slots, slots)] for i in range(4)]
    loads = [
        pltpu.make_async_copy(source.at[place], target, loaded.at[i])
        for i, (source, place, target) in enumerate(zip(sources, places, targets))
    ]
    for load in loads:
        load.start()
    stores = [
        pltpu.make_async_copy(results.at[i], target, stored.at[i])
        for i, target in enumerate((other_ref, own_ref))
    ]
    for load in loads[:4]:
        load.wait()
    total = outer_product(near[:, part:], acts[:slots])
    total += outer_product(rows[: 2 * slots, part:], acts[slots : 3 * slots])
    results[0] = total.astype(BF16)
    stores[0].start()
    loads[4].wait()
    total = outer_product(near[:, :part], acts[:slots])
    total += outer_product(rows[:, :part], acts[slots:])
    results[1] = total.astype(BF16)
    stores[1].start()
    for store in stores:
        store.wait()


def down_call(rows, near, acts, after):
    sources = [near, *acts]
    arrays = [array for array, _ in sources]
    places = [place for _, place in sources]
    slots, hidden_width = arrays[1].shape[1:]
    width = rows.shape[1]
    return pl.pallas_call(
        functools.partial(down_kernel, places, len(after)),
        in_specs=[pl.BlockSpec(memory_space=pltpu.VMEM)]
        + [ANYWHERE] * (len(arrays) + len(after)),
        out_specs=[ANYWHERE] * 2,
        out_shape=[jax.ShapeDtypeStruct((width // 2, hidden_width), BF16)] * 2,
        scratch_shapes=[
            pltpu.VMEM((slots, width), BF16),
            pltpu.VMEM((4 * slots, hidden_width), BF16),
            pltpu.VMEM((2, width // 2, hidden_width), BF16),
            pltpu.SemaphoreType.DMA((5,)),
            pltpu.SemaphoreType.DMA((2,)),
        ],
        compiler_params=pltpu.CompilerParams(vmem_limit_bytes=50 * MIB),
        cost_estimate=SMALL,
        name="down_terms",
    )(pltpu.with_memory_space_constraint(rows, pltpu.VMEM), *arrays, *after)


def router_kernel(total_experts, n_after, products, places, weights, gate, inputs, *refs):
    input_ref, part_ref = refs[n_after:]
    by_slot = products[...]
    capacity = by_slot.shape[1]
    slots = lax.broadcasted_iota(jnp.int32, (capacity, places.shape[1]), 0).astype(F32)
    sums = []
    for expert in range(total_experts):
        hit = slots == places[expert : expert + 1, :]
        sums.append(
            jnp.sum(jnp.where(hit, by_slot[expert][:, None], 0.0), axis=0, keepdims=True)
        )
    pair_sums = jnp.concatenate(sums, axis=0)
    logits = pair_sums - weights[...] * jnp.sum(pair_sums, axis=0, keepdims=True)
    dense = jnp.where(places[...] >= 0.0, logits, 0.0).astype(BF16)
    step = part_ref.shape[2]
    for index in range(part_ref.shape[0]):
        columns = inputs[:, index * step : (index + 1) * step]
        part_ref[index] = jnp.dot(dense, columns, preferred_element_type=F32)
    input_ref[...] = lax.dot_general(
        dense, gate[...], (((0,), (0,)), ((), ())), preferred_element_type=F32
    ).astype(BF16)


def router_call(products, places, weights, gate, inputs, after):
    vmem = pl.BlockSpec(memory_space=pltpu.VMEM)
    return pl.pallas_call(
        functools.partial(router_kernel, gate.shape[0], len(after)),
        in_specs=[vmem] * 5 + [ANYWHERE] * len(after),
        out_specs=[vmem] * 2,
        out_shape=[
            jax.ShapeDtypeStruct(inputs.shape, BF16),
            jax.ShapeDtypeStruct((8, gate.shape[0], gate.shape[1] // 8), F32),
        ],
        compiler_params=pltpu.CompilerParams(vmem_limit_bytes=24 * MIB),
        cost_estimate=SMALL,
        name="router_terms",
    )(products, places, weights, gate, inputs, *after)


def sum_kernel(*refs):
    own, first, second, third = refs[:4]
    refs[-1][...] = (own[...] + first[...]) + (second[...] + third[...])


def sum_planes(x, others, after):
    vmem = pl.BlockSpec(memory_space=pltpu.VMEM)
    return pl.pallas_call(
        sum_kernel,
        in_specs=[vmem] * 4 + [ANYWHERE] * len(after),
        out_specs=vmem,
        out_shape=jax.ShapeDtypeStruct(x.shape, x.dtype),
        cost_estimate=SMALL,
        name="sum_planes",
    )(x, *others, *after)


def local_line(inputs, out_grad, combine, routes, saved_hidden, down_weight, router_weight):
    width = out_grad.shape[1]
    local_experts = down_weight.shape[0]
    total_experts = router_weight.shape[0]
    capacity = saved_hidden.shape[3]
    hidden_width = saved_hidden.shape[4]
    slots = 8 * capacity
    part = width // 4
    plane = lax.axis_index("dp")
    member = lax.axis_index("expert")
    lower = plane < 2
    acts = saved_hidden.reshape(local_experts, slots, hidden_width)

    routed, positions, weights = dense_routes(routes, combine, total_experts)
    notes = describe(positions, weights)
    parts = [out_grad[:, i * part : (i + 1) * part] for i in range(4)]

    pair = jnp.concatenate(
        [jnp.where(lower, parts[2], parts[1]), jnp.where(lower, parts[3], parts[0]), notes], axis=1
    )
    single = jnp.concatenate([jnp.where(lower, parts[1], parts[2]), notes], axis=1)
    from_inner = lax.ppermute(pair, "dp", INNER)
    from_far = lax.ppermute(pair, "dp", FAR)
    from_outer = lax.ppermute(single, "dp", OUTER)

    other_part = jnp.where(lower, 0, 3)
    place = jnp.stack([member, plane, other_part]).astype(jnp.int32)

    tokens = jnp.concatenate([out_grad, notes], axis=1)
    across = plane_swap(tokens, 2)
    along = plane_swap(tokens, 4)
    n_tokens = tokens.shape[0]
    half = n_tokens // 2

    groups = [(0, 2), (2, local_experts)]
    acts_early, *acts_late = copies(
        "acts_pieces",
        [acts],
        [(stop - start, slots, hidden_width) for start, stop in groups],
        [[(0, slice(start, stop), Ellipsis)] for start, stop in groups],
        [across],
        60 * MIB,
    )
    *halves, stacked = copies(
        "first_pieces",
        [across, along, tokens],
        [(half, tokens.shape[1])] * 2 + [(3, *tokens.shape)],
        [[(0, rows_of(0, half), Ellipsis)], [(1, rows_of(half, n_tokens), Ellipsis)]]
        + [[(source, Ellipsis, index) for index, source in enumerate((2, 0, 1))]],
        [from_inner, from_far, from_outer, acts_early],
        60 * MIB,
    )
    diagonal = plane_diagonal(halves)
    own_blocks = plane_blocks(tokens, across, along, stacked, diagonal)
    inners = [lax.ppermute(acts_early, "dp", INNER)]
    outers = [lax.ppermute(acts_early, "dp", OUTER)]

    widths = [block.shape[1] for block in (from_inner, from_far, from_outer)]
    starts = [sum(widths[:i]) for i in range(3)]
    (columns,) = copies(
        "side_by_side",
        [from_inner, from_far, from_outer],
        [(n_tokens, sum(widths))],
        [[(i, Ellipsis, columns_of(starts[i], starts[i] + widths[i])) for i in range(3)]],
        diagonal,
        60 * MIB,
    )
    columns_across = plane_swap(columns, 2)
    columns_along = plane_swap(columns, 4)

    hidden, products, near, *late = hidden_call(
        place, own_blocks, down_weight, acts, total_experts, capacity, part,
        [columns], acts_late,
    )
    inners += [lax.ppermute(a, "dp", INNER) for a in late]
    outers += [lax.ppermute(a, "dp", OUTER) for a in late]
    fars = [lax.ppermute(outers[0], "dp", INNER)]
    fars += [
        lax.ppermute(outers[1][i : i + 1], "dp", INNER) for i in range(local_experts - 2)
    ]

    *column_halves, stacked = copies(
        "second_pieces",
        [columns_across, columns_along, columns],
        [(half, sum(widths))] * 2 + [(3, *columns.shape)],
        [[(0, rows_of(0, half), Ellipsis)], [(1, rows_of(half, n_tokens), Ellipsis)]]
        + [[(source, Ellipsis, index) for index, source in enumerate((2, 0, 1))]],
        [hidden, outers[0], inners[0]],
        56 * MIB,
    )
    (products,) = held_until([products], column_halves)
    returned = lax.all_to_all(
        products.transpose(1, 0, 2), "expert", split_axis=0, concat_axis=0
    ).reshape(total_experts, LANES)
    input_grad, router_part = router_call(
        returned, positions.T, weights.T, router_weight, inputs, []
    )
    corner = held_until(plane_diagonal(column_halves), [router_part])
    other_blocks = plane_blocks(columns, columns_across, columns_along, stacked, corner)
    rows = rows_call(
        place, other_blocks, (2 * part, 2 * part, part), local_experts, total_experts, capacity, []
    )

    def down(expert, after, hold=()):
        group, place = divmod(expert, 2)
        far = (fars[0], expert) if expert < 2 else (fars[expert - 1], 0)
        pieces = [(acts, expert), (inners[group], place), far, (outers[group], place)]
        own, other = down_call(rows[expert], (near, expert), pieces, after)
        if hold:
            (other,) = held_until([other], hold)
        return own, lax.ppermute(other, "dp", OUTWARD)

    def finish(own, came):
        return (own.astype(F32) + came.astype(F32)).astype(BF16)

    downs = [down(0, [])]
    downs.append(down(1, [downs[0][0]]))
    reduced = jnp.sum(
        lax.all_to_all(router_part, "expert", split_axis=0, concat_axis=0), axis=0
    )
    downs.append(down(2, [downs[1][0], inners[1], downs[0][1]]))
    others = [lax.ppermute(reduced, "dp", [(i, i ^ k) for i in range(4)]) for k in (1, 2, 3)]
    finished = [finish(*downs[0])]
    downs.append(down(3, [downs[2][0], *finished, *others]))
    finished += [finish(*downs[expert]) for expert in range(1, 4)]
    summed = sum_planes(reduced, others, [downs[-1][0]])
    router_grad = (
        lax.all_gather(summed, "expert").transpose(1, 0, 2).reshape(total_experts, width)
    )

    down_grad = jnp.stack(finished)

    hidden_grad = hidden.reshape(saved_hidden.shape)
    return (hidden_grad, down_grad, input_grad, router_grad)


def solution(mesh):
    in_line = mesh.shape["dp"] == 4 and mesh.shape["expert"] == 8

    def local(inputs, out_grad, combine, routes, saved_hidden, down_weight, router_weight):
        tokens, width = out_grad.shape
        fits = (
            in_line
            and tokens == LANES
            and KINDS * router_weight.shape[0] == LANES
            and width % 2048 == 0
            and saved_hidden.shape[3] % 16 == 0
            and saved_hidden.shape[4] % LANES == 0
        )
        body = local_line if fits else local_any
        return body(
            inputs, out_grad, combine, routes, saved_hidden, down_weight, router_weight
        )

    placed = (
        P(("dp", "expert"), None),
        P(("dp", "expert"), None),
        P(("dp", "expert"), None),
        P(("dp", "expert"), None),
        P("dp", "expert", None, None, None),
        P("expert", None, None),
        P(),
    )
    return jax.shard_map(
        local,
        mesh=mesh,
        in_specs=placed,
        out_specs=(
            P("dp", "expert", None, None, None),
            P("expert", "dp", None),
            P(("dp", "expert"), None),
            P(),
        ),
        check_vma=False,
    )
```
